32 devices in a mesh: brick: 8 (over y, x, core), chan: 4 (over z).
Axes of the slice: x: 2, y: 2, z: 4, core: 2. Of those that a mesh axis runs over, the one named last changes fastest.
Arguments:
- node_x: bfloat16 [49, 128, 1024], P(None, 'chan', 'brick'), may hold values from -6 to 6
- cotangent: bfloat16 [49, 128, 1024], P(None, 'chan', 'brick'), may hold values from -6 to 6
- wigner: bfloat16 [235, 8192], P(None, 'brick'), may hold values from -4 to 4
- src_index: int32 [8192], P('brick'), may hold values from 0 to 191
- dst_index: int32 [8192], P('brick'), may hold values from 0 to 127
- edge_scale: float32 [8192], P('brick'), may hold values from 0.1 to 1
- edge_count: int32 [8], P('brick'), may hold values from 341 to 1024, as said below
- w_zero: bfloat16 [7, 128, 7, 128], P(None, 'chan'), may hold values from -0.1875 to 0.1875
- w_one: bfloat16 [2, 6, 128, 6, 128], P(None, None, 'chan'), may hold values from -0.15625 to 0.15625
- w_two: bfloat16 [2, 5, 128, 5, 128], P(None, None, 'chan'), may hold values from -0.15625 to 0.15625
Outputs:
- grad_x: float32 [49, 128, 1024], P(None, 'chan', 'brick')
- grad_w_zero: float32 [7, 128, 7, 128], P(None, 'chan', None, 'brick')
- grad_w_one: float32 [2, 6, 128, 6, 128], P(None, None, 'chan', None, 'brick')
- grad_w_two: float32 [2, 5, 128, 5, 128], P(None, None, 'chan', None, 'brick')
The draws below stay inside these ranges and needn't reach their ends.
Inputs may be any that keep to these rules, and one draw needn't show every extreme that they name: Slots 0 to edge_count[b] - 1 of brick b hold edges, the rest are padding; one brick's list is full.
All inputs are finite; a program needn't handle non-finite values.
Results may differ from the reference program's by a relative error of at most 0.0065.
Values may be sent and summed in bfloat16 or wider, within the bound.
A program may use at most 64 MiB of HBM per device.

```python
import jax
import jax.numpy as jnp
import numpy as np
from jax import lax

C = 128
COEF = 49
ROT = 235
L0 = 7
L1 = 6
L2 = 5
A_DEV = 128
RIM = 32
EDGE_CAP = 1024
BRICKS = 8
ATOMS = 1024
EDGES = 8192


def wigner_scales():
    scales = []
    for degree in range(7):
        max_order = min(degree, 2)
        span_cols = 2 * degree + 1
        scales += [span_cols ** (-0.5)] * ((2 * max_order + 1) * span_cols)
    return np.array(scales, dtype=np.float32)


def draw_wigner(key, part):
    key = jax.random.fold_in(key, 11)
    scales = jnp.asarray(wigner_scales())[:, None]
    samples = jnp.clip(jax.random.normal(key, (ROT, EDGES), jnp.float32), -4.0, 4.0)
    return (samples * scales).astype(jnp.bfloat16)


def draw_edge_count(key, part):
    key = jax.random.fold_in(key, 5)
    key_counts, key_full = jax.random.split(key)
    counts = jax.random.randint(key_counts, (BRICKS,), EDGE_CAP // 3, EDGE_CAP // 2 + 1, jnp.int32)
    fullest = jax.random.randint(key_full, (), 0, BRICKS, jnp.int32)
    return jnp.where(jnp.arange(BRICKS, dtype=jnp.int32) == fullest, EDGE_CAP, counts).astype(jnp.int32)


def set_ends(result, key, low, largest):
    spot = [jax.random.randint(jax.random.fold_in(key, axis), (), 0, length) for axis, length in enumerate(result.shape)]
    longest = result.shape.index(max(result.shape))
    neighbour = spot[:longest] + [(spot[longest] + 1) % result.shape[longest]] + spot[longest + 1:]
    return result.at[tuple(spot)].set(low).at[tuple(neighbour)].set(largest)


def block_scale(stream_key, extent, shards, low, top_value):
    def one(dim, blocks):
        steps = jax.random.uniform(jax.random.fold_in(jax.random.fold_in(stream_key, 6), dim), (blocks,), jnp.float32, low / len(shards), top_value / len(shards))
        return jnp.repeat(jnp.exp(steps), extent[dim] // blocks).reshape((-1,) + (1,) * (len(extent) - dim - 1))

    gain = one(*shards[0])
    for cut in shards[1:]:
        gain = gain * one(*cut)
    return gain


def normal_values(rng, shape, width, limit, cuts=(), held_as=jnp.bfloat16):
    entries = width * jax.random.normal(rng, shape, jnp.float32)
    if cuts:
        entries = entries * block_scale(rng, shape, cuts, -0.22, 0.18)
    return jnp.clip(entries, -limit, limit).astype(held_as)


def setup_inputs(seed: int = 0) -> dict:
    seeds = jax.random.split(jax.random.key(seed), 11)
    return {
        "node_x": normal_values(seeds[0], (COEF, C, ATOMS), 1.0, 6.0, ((1, 4), (2, 8))),
        "cotangent": normal_values(seeds[1], (COEF, C, ATOMS), 1.0, 6.0, ((1, 4), (2, 8))),
        "wigner": draw_wigner(jax.random.fold_in(seeds[10], 71), 0),
        "src_index": set_ends(jax.random.randint(seeds[3], (EDGES,), 0, A_DEV + 2 * RIM), jax.random.fold_in(seeds[3], 1), 0, (A_DEV + 2 * RIM) - 1).astype(jnp.int32),
        "dst_index": set_ends(jax.random.randint(seeds[4], (EDGES,), 0, A_DEV), jax.random.fold_in(seeds[4], 1), 0, A_DEV - 1).astype(jnp.int32),
        "edge_scale": jnp.clip(0.1 + 0.9 * jax.random.uniform(seeds[5], (EDGES,), jnp.float32) ** block_scale(seeds[5], (EDGES,), ((0, 8),), -0.2, 0.2), 0.1, 1.0),
        "edge_count": draw_edge_count(jax.random.fold_in(seeds[10], 71), 0),
        "w_zero": normal_values(seeds[7], (L0, C, L0, C), (L0 * C) ** -0.5, 0.1875, ((1, 4),)),
        "w_one": normal_values(seeds[8], (2, L1, C, L1, C), (2 * L1 * C) ** -0.5, 0.15625, ((2, 4),)),
        "w_two": normal_values(seeds[9], (2, L2, C, L2, C), (2 * L2 * C) ** -0.5, 0.15625, ((2, 4),)),
    }


def kept_row(degree, azimuth):
    if azimuth == 0:
        return degree
    if azimuth == 1:
        return 6 + degree
    if azimuth == -1:
        return 12 + degree
    if azimuth == 2:
        return 17 + degree
    return 22 + degree


def to_edge_frame(values, wigner):
    kept_rows = [None] * 29
    offset = 0
    for degree in range(7):
        max_order = min(degree, 2)
        span_cols = 2 * degree + 1
        for azimuth in range(-max_order, max_order + 1):
            running = jnp.zeros(values.shape[1:], jnp.float32)
            for column in range(span_cols):
                factor = wigner[offset + (azimuth + max_order) * span_cols + column].astype(jnp.float32)
                running = running + factor[None, :] * values[degree * degree + column].astype(jnp.float32)
            kept_rows[kept_row(degree, azimuth)] = running
        offset += (2 * max_order + 1) * span_cols
    return jnp.stack(kept_rows)


def from_edge_frame(kept_rows, wigner):
    full_rows = []
    offset = 0
    for degree in range(7):
        max_order = min(degree, 2)
        span_cols = 2 * degree + 1
        for column in range(span_cols):
            running = jnp.zeros(kept_rows.shape[1:], jnp.float32)
            for azimuth in range(-max_order, max_order + 1):
                factor = wigner[offset + (azimuth + max_order) * span_cols + column].astype(jnp.float32)
                running = running + factor[None, :] * kept_rows[kept_row(degree, azimuth)]
            full_rows.append(running)
        offset += (2 * max_order + 1) * span_cols
    return jnp.stack(full_rows)


def contract(weights, grads):
    return lax.dot_general(weights.astype(jnp.float32), grads.astype(jnp.float32),
                           (((2, 3), (0, 1)), ((), ())), precision=lax.Precision.HIGHEST)


def outer(inputs, grads):
    return lax.dot_general(inputs.astype(jnp.float32), grads.astype(jnp.float32),
                           (((2,), (2,)), ((), ())), precision=lax.Precision.HIGHEST)


def so2_back(w_zero, w_one, w_two, edge_grad, edge_in):
    back_rows = [contract(w_zero, edge_grad[0:7])]
    term_zero = outer(edge_in[0:7], edge_grad[0:7])
    weight_terms = []
    for weights, bottom, middle, ceiling in ((w_one, 7, 13, 19), (w_two, 19, 24, 29)):
        grad_plus = edge_grad[bottom:middle]
        grad_minus = edge_grad[middle:ceiling]
        in_plus = edge_in[bottom:middle]
        in_minus = edge_in[middle:ceiling]
        back_rows.append(contract(weights[0], grad_plus) + contract(weights[1], grad_minus))
        back_rows.append(contract(weights[0], grad_minus) - contract(weights[1], grad_plus))
        weight_terms.append(jnp.stack([outer(in_plus, grad_plus) + outer(in_minus, grad_minus),
                                       outer(in_plus, grad_minus) - outer(in_minus, grad_plus)]))
    return jnp.concatenate(back_rows, axis=0), term_zero, weight_terms[0], weight_terms[1]


def reference(node_x, cotangent, wigner, src_index, dst_index, edge_scale, edge_count, w_zero, w_one, w_two):
    rim_len = A_DEV // 4
    position = lax.iota(jnp.int32, EDGE_CAP)

    def brick_step(folded, brick_idx):
        grad_x, sum_zero, sum_one, sum_two = folded
        first_slot = (brick_idx * EDGE_CAP).astype(jnp.int32)
        src_here = lax.dynamic_slice_in_dim(src_index, first_slot, EDGE_CAP)
        dst_here = lax.dynamic_slice_in_dim(dst_index, first_slot, EDGE_CAP)
        scale_here = lax.dynamic_slice_in_dim(edge_scale, first_slot, EDGE_CAP)
        wig_here = lax.dynamic_slice_in_dim(wigner, first_slot, EDGE_CAP, 1)
        count_here = lax.dynamic_slice_in_dim(edge_count, brick_idx, 1)[0]
        base_atom = brick_idx * A_DEV
        src_atom = ((base_atom + src_here - rim_len + ATOMS) % ATOMS).astype(jnp.int32)
        dst_atom = (base_atom + dst_here).astype(jnp.int32)
        factor = jnp.where(position < count_here, 0.25 * scale_here, 0.0)
        edge_grad = (to_edge_frame(jnp.take(cotangent, dst_atom, axis=2), wig_here) * factor).astype(jnp.bfloat16)
        edge_in = to_edge_frame(jnp.take(node_x, src_atom, axis=2), wig_here).astype(jnp.bfloat16)
        back_rows, term_zero, term_one, term_two = so2_back(w_zero, w_one, w_two, edge_grad, edge_in)
        full_rows = from_edge_frame(back_rows, wig_here)
        grad_x = grad_x.at[:, :, src_atom].add(full_rows)
        return (grad_x, sum_zero + term_zero, sum_one + term_one, sum_two + term_two), None

    initial = (jnp.zeros((COEF, C, ATOMS), jnp.float32),
               jnp.zeros((L0, C, L0, C), jnp.float32),
               jnp.zeros((2, L1, C, L1, C), jnp.float32),
               jnp.zeros((2, L2, C, L2, C), jnp.float32))
    folded, ignored = lax.scan(brick_step, initial, jnp.arange(BRICKS, dtype=jnp.int32))
    return folded[0], folded[1], folded[2], folded[3]
```

```python
import functools

import jax
import jax.numpy as jnp
from jax import lax
from jax.experimental import pallas as pl
from jax.experimental.pallas import tpu as pltpu
from jax.sharding import PartitionSpec as P

LANES = 128
VMEM_BYTES = 48 * 1024 * 1024
MESH = pl.DeviceIdType.MESH
NT = (((1,), (1,)), ((), ()))
NN = (((1,), (0,)), ((), ()))


def degree_offset(degree):
    return sum((2 * min(k, 2) + 1) * (2 * k + 1) for k in range(degree))


def rotate_tile(load, wig, store):
    for degree in range(7):
        top = min(degree, 2)
        span = 2 * degree + 1
        offset = degree_offset(degree)
        sums = [None] * (2 * top + 1)
        for column in range(span):
            value = load(degree * degree + column)
            for m in range(2 * top + 1):
                term = wig(offset + m * span + column) * value
                sums[m] = term if sums[m] is None else sums[m] + term
        for m in range(2 * top + 1):
            store(kept_row(degree, m - top), sums[m])


def unrotate_tile(load, wig, store):
    for degree in range(7):
        top = min(degree, 2)
        span = 2 * degree + 1
        offset = degree_offset(degree)
        rows = [load(kept_row(degree, m - top)) for m in range(2 * top + 1)]
        for column in range(span):
            total = None
            for m in range(2 * top + 1):
                term = wig(offset + m * span + column) * rows[m]
                total = term if total is None else total + term
            store(degree * degree + column, total)


def source_onehot(src, rows, rim):
    own = rows // 2
    place = jnp.where(src < rim, src + own, jnp.where(src < rim + own, src - rim, src))
    return (lax.broadcasted_iota(jnp.int32, (rows, src.shape[1]), 0) == place).astype(jnp.bfloat16)


def edge_in_kernel(chan, rim, src_ref, wig_ref, ext_ref, out_ref, wide, gathered):
    width = out_ref.shape[1]
    wide[...] = wig_ref[...].astype(jnp.float32)
    onehot = source_onehot(src_ref[...], ext_ref.shape[1], rim)
    gathered[...] = lax.dot_general(ext_ref[...], onehot, NN, preferred_element_type=jnp.float32)

    def lanes_step(t, carry):
        at = pl.ds(pl.multiple_of(t * LANES, LANES), LANES)

        def store(row, tile):
            out_ref[row * chan : (row + 1) * chan, at] = tile.astype(jnp.bfloat16)

        rotate_tile(
            lambda i: gathered[i * chan : (i + 1) * chan, at], lambda k: wide[k : k + 1, at], store
        )
        return carry

    lax.fori_loop(0, width // LANES, lanes_step, 0)


def edge_kernel(
    chan, piece, rim, count_ref, src_ref, dst_ref, scale_ref, wig_ref, cot_ref, in_ref,
    wz_ref, w1_ref, w2_ref, part_ref, own_ref, rim_ref,
    wide, scaled, gathered, g0, g1, g2, back, full, a0, a1, a2, gx,
):
    step = pl.program_id(0)
    width = src_ref.shape[1]
    shards = cot_ref.shape[0]
    halves = chan // piece

    @pl.when(step == 0)
    def _():
        for ref in (a0, a1, a2, gx):
            ref[...] = jnp.zeros_like(ref)

    position = step * width + lax.broadcasted_iota(jnp.int32, (1, width), 1)
    factor = jnp.where(position < count_ref[0], 0.25 * scale_ref[...], 0.0)
    wide[...] = wig_ref[...].astype(jnp.float32)
    scaled[...] = wide[...] * factor
    atoms = cot_ref.shape[2]
    onehot = (
        lax.broadcasted_iota(jnp.int32, (atoms, width), 0) == dst_ref[...]
    ).astype(jnp.bfloat16)

    def shard_step(s, carry):
        gathered[...] = lax.dot_general(cot_ref[s], onehot, NN, preferred_element_type=jnp.float32)

        def lanes_step(t, inner):
            at = pl.ds(pl.multiple_of(t * LANES, LANES), LANES)

            def store(row, tile):
                tile = tile.astype(jnp.bfloat16)
                for h in range(halves):
                    if row < 7:
                        ref, high, index = g0, 7, row
                    elif row < 19:
                        ref, high, index = g1.at[(row - 7) // 6], 6, (row - 7) % 6
                    else:
                        ref, high, index = g2.at[(row - 19) // 5], 5, (row - 19) % 5
                    first = pl.multiple_of(
                        (s * halves + h) * (high * piece) + index * piece, piece
                    )
                    ref[pl.ds(first, piece), at] = tile[h * piece : (h + 1) * piece]

            rotate_tile(
                lambda i: gathered[i * chan : (i + 1) * chan, at],
                lambda k: scaled[k : k + 1, at],
                store,
            )
            return inner

        lax.fori_loop(0, width // LANES, lanes_step, 0)
        return carry

    lax.fori_loop(0, shards, shard_step, 0)

    def dot(a, b, dims):
        return lax.dot_general(a, b, dims, preferred_element_type=jnp.float32)

    back[0 : 7 * chan] = dot(wz_ref[...], g0[...], NN)
    a0[...] += dot(g0[...], in_ref[0 : 7 * chan], NT)
    for w, g, a, first, high in ((w1_ref, g1, a1, 7, 6), (w2_ref, g2, a2, 19, 5)):
        low, middle, top = first * chan, (first + high) * chan, (first + 2 * high) * chan
        plus, minus = in_ref[low:middle], in_ref[middle:top]
        back[low:middle] = dot(w[0], g[0], NN) + dot(w[1], g[1], NN)
        back[middle:top] = dot(w[0], g[1], NN) - dot(w[1], g[0], NN)
        a[0] += dot(g[0], plus, NT) + dot(g[1], minus, NT)
        a[1] += dot(g[1], plus, NT) - dot(g[0], minus, NT)

    def back_step(t, carry):
        at = pl.ds(pl.multiple_of(t * LANES, LANES), LANES)

        def store(i, tile):
            full[i * chan : (i + 1) * chan, at] = tile.astype(jnp.bfloat16)

        unrotate_tile(
            lambda r: back[r * chan : (r + 1) * chan, at], lambda k: wide[k : k + 1, at], store
        )
        return carry

    lax.fori_loop(0, width // LANES, back_step, 0)
    gx[...] += dot(full[...], source_onehot(src_ref[...], gx.shape[1], rim), NT)

    @pl.when(step == pl.num_programs(0) - 1)
    def _():
        own_ref[...] = gx[:, :atoms]
        rim_ref[...] = gx[:, atoms:].astype(jnp.bfloat16)
        part_ref[...] = jnp.zeros_like(part_ref)
        for b in range(part_ref.shape[0]):
            row = 0
            for a, high in ((a0, 7), (a1.at[0], 6), (a1.at[1], 6), (a2.at[0], 5), (a2.at[1], 5)):
                rows = high * piece
                part_ref[b, row : row + rows, : high * chan] = a[b * rows : (b + 1) * rows].astype(
                    jnp.bfloat16
                )
                row += rows


def sum_kernel(
    bricks, rim, part_ref, own_ref, rim_ref, sum_ref, gx_ref,
    near, far, outgoing, from_next, from_prev, send1, recv1, send2, recv2, sendx, recvx,
):
    me = lax.axis_index("brick")
    core = lax.rem(me, 2)
    mine = lax.div(me, 2)
    pairs = bricks // 2
    sibling = me + 1 - 2 * core
    barrier = pltpu.get_barrier_semaphore()
    for d in range(1, bricks):
        pl.semaphore_signal(
            barrier, inc=1, device_id={"brick": lax.rem(me + d, bricks)}, device_id_type=MESH
        )
    pl.semaphore_wait(barrier, bricks - 1)

    def remote(src, dst, send, recv, to):
        copy = pltpu.make_async_remote_copy(
            src_ref=src, dst_ref=dst, send_sem=send, recv_sem=recv,
            device_id={"brick": to}, device_id_type=MESH,
        )
        copy.start()
        return copy

    order = [d for d in range(pairs - 1, 0, -1)] + [0]
    first = []
    for d in order:
        q = lax.rem(mine + d, pairs)
        first.append(
            remote(part_ref.at[2 * q + (1 - core)], near.at[q], send1.at[d], recv1.at[d], sibling)
        )
    following = lax.rem(me + 1, bricks)
    previous = lax.rem(me + bricks - 1, bricks)
    edges = [
        remote(rim_ref, from_next, sendx.at[0], recvx.at[0], previous),
        remote(rim_ref, from_prev, sendx.at[1], recvx.at[1], following),
    ]
    second = []
    for copy, d in zip(first, order):
        copy.wait_recv()
        q = lax.rem(mine + d, pairs)
        both = part_ref[2 * q + core].astype(jnp.float32) + near[q].astype(jnp.float32)
        if d:
            outgoing[d] = both.astype(jnp.bfloat16)
            second.append(
                remote(outgoing.at[d], far.at[d], send2.at[d], recv2.at[d], 2 * q + core)
            )
        else:
            sum_ref[...] = both
    for copy in edges:
        copy.wait_recv()
    lane = lax.broadcasted_iota(jnp.int32, from_next.shape, 1)
    arrived = jnp.where(
        lane < rim,
        from_next[...].astype(jnp.float32),
        jnp.where(lane < 2 * rim, from_prev[...].astype(jnp.float32), 0.0),
    )
    gx_ref[...] = own_ref[...] + pltpu.roll(arrived, from_next.shape[1] - rim, 1)
    for copy, d in zip(second, order):
        copy.wait_recv()
        sum_ref[...] += far[d].astype(jnp.float32)
    for copy in first + second + edges:
        copy.wait_send()


def whole():
    return pl.BlockSpec(memory_space=pltpu.VMEM)


def kernel_body(
    node_x, cotangent, wigner, src_index, dst_index, edge_scale, edge_count, w_zero, w_one, w_two
):
    bricks, shards = lax.axis_size("brick"), lax.axis_size("chan")
    coef, chan, atoms = node_x.shape
    total = w_zero.shape[3]
    piece = total // bricks
    rim = atoms // 4
    slots = src_index.shape[0]
    entries = wigner.shape[0]
    width = 256
    steps = slots // width
    f32, bf16 = jnp.float32, jnp.bfloat16

    full_cot = lax.all_gather(cotangent.reshape(coef * chan, atoms), "chan")

    up = [(i, (i + 1) % bricks) for i in range(bricks)]
    down = [(j, i) for i, j in up]
    before = lax.ppermute(node_x[:, :, atoms - rim :], "brick", up)
    after = lax.ppermute(node_x[:, :, :rim], "brick", down)
    ext = jnp.concatenate(
        [node_x, before, after, jnp.zeros((coef, chan, atoms - 2 * rim), bf16)], axis=2
    ).reshape(coef * chan, 2 * atoms)

    src = src_index.reshape(1, slots)
    dst = dst_index.reshape(1, slots)
    scale = edge_scale.reshape(1, slots)
    row_spec = pl.BlockSpec((1, width), lambda i: (0, i))
    wig_spec = pl.BlockSpec((entries, width), lambda i: (0, i))
    in_spec = pl.BlockSpec((29 * chan, width), lambda i: (0, i))
    fma = entries * chan * slots * 2
    edge_in = pl.pallas_call(
        functools.partial(edge_in_kernel, chan, rim),
        grid=(steps,),
        out_shape=jax.ShapeDtypeStruct((29 * chan, slots), bf16),
        in_specs=[row_spec, wig_spec, whole()],
        out_specs=in_spec,
        scratch_shapes=[
            pltpu.VMEM((entries, width), f32),
            pltpu.VMEM((coef * chan, width), f32),
        ],
        compiler_params=pltpu.CompilerParams(vmem_limit_bytes=VMEM_BYTES),
        cost_estimate=pl.CostEstimate(flops=fma * 40, bytes_accessed=4 << 20, transcendentals=0),
        name="edge_in",
    )(src, wigner, ext)

    def columns(w, high):
        lead = w.shape[:-4]
        w = w.reshape(lead + (high, chan, high, bricks, piece))
        return jnp.swapaxes(w, -3, -2).reshape(lead + (high * chan, high * total))

    wz, w1, w2 = columns(w_zero, 7), columns(w_one, 6), columns(w_two, 5)
    rows = (7 + 12 + 10) * piece
    part, own, rim_part = pl.pallas_call(
        functools.partial(edge_kernel, chan, piece, rim),
        grid=(steps,),
        out_shape=(
            jax.ShapeDtypeStruct((bricks, rows, 2 * LANES), bf16),
            jax.ShapeDtypeStruct((coef * chan, atoms), f32),
            jax.ShapeDtypeStruct((coef * chan, atoms), bf16),
        ),
        in_specs=[
            pl.BlockSpec(memory_space=pltpu.SMEM), row_spec, row_spec, row_spec, wig_spec,
            whole(), in_spec, whole(), whole(), whole(),
        ],
        out_specs=(whole(), whole(), whole()),
        scratch_shapes=[
            pltpu.VMEM((entries, width), f32),
            pltpu.VMEM((entries, width), f32),
            pltpu.VMEM((coef * chan, width), f32),
            pltpu.VMEM((7 * total, width), bf16),
            pltpu.VMEM((2, 6 * total, width), bf16),
            pltpu.VMEM((2, 5 * total, width), bf16),
            pltpu.VMEM((29 * chan, width), f32),
            pltpu.VMEM((coef * chan, width), bf16),
            pltpu.VMEM((7 * total, 7 * chan), f32),
            pltpu.VMEM((2, 6 * total, 6 * chan), f32),
            pltpu.VMEM((2, 5 * total, 5 * chan), f32),
            pltpu.VMEM((coef * chan, 2 * atoms), f32),
        ],
        compiler_params=pltpu.CompilerParams(vmem_limit_bytes=VMEM_BYTES),
        cost_estimate=pl.CostEstimate(
            flops=fma * 200, bytes_accessed=8 << 20, transcendentals=0
        ),
        name="edges",
    )(edge_count, src, dst, scale, wigner, full_cot, edge_in, wz, w1, w2)

    pairs = bricks // 2
    dma = pltpu.SemaphoreType.DMA
    sums, grad_x = pl.pallas_call(
        functools.partial(sum_kernel, bricks, rim),
        out_shape=(
            jax.ShapeDtypeStruct((rows, 2 * LANES), f32),
            jax.ShapeDtypeStruct((coef * chan, atoms), f32),
        ),
        in_specs=[whole()] * 3,
        out_specs=(whole(), whole()),
        scratch_shapes=[
            pltpu.VMEM((pairs, rows, 2 * LANES), bf16),
            pltpu.VMEM((pairs, rows, 2 * LANES), bf16),
            pltpu.VMEM((pairs, rows, 2 * LANES), bf16),
            pltpu.VMEM((coef * chan, atoms), bf16),
            pltpu.VMEM((coef * chan, atoms), bf16),
            dma((pairs,)), dma((pairs,)), dma((pairs,)), dma((pairs,)), dma((2,)), dma((2,)),
        ],
        compiler_params=pltpu.CompilerParams(
            vmem_limit_bytes=VMEM_BYTES, collective_id=0, has_side_effects=True
        ),
        name="sums",
    )(part, own, rim_part)

    def columns_back(first, high):
        block = sums[first : first + high * piece, : high * chan]
        return block.reshape(high, piece, high, chan).transpose(2, 3, 0, 1)

    ends = [0, 7 * piece, 13 * piece, 19 * piece, 24 * piece]
    return (
        grad_x.reshape(coef, chan, atoms),
        columns_back(ends[0], 7),
        jnp.stack([columns_back(ends[1], 6), columns_back(ends[2], 6)]),
        jnp.stack([columns_back(ends[3], 5), columns_back(ends[4], 5)]),
    )


def padded(x, sides, width):
    for axis, dim in sides:
        devices, length = (lax.axis_size(axis), x.shape[dim])
        up = [(i, (i + 1) % devices) for i in range(devices)]
        down = [(j, i) for i, j in up]
        last = lax.slice_in_dim(x, length - width, length, axis=dim)
        initial = lax.slice_in_dim(x, 0, width, axis=dim)
        before = lax.ppermute(last, axis, up)
        after = lax.ppermute(initial, axis, down)
        x = jnp.concatenate([before, x, after], axis=dim)
    return x


def passed_along(block, axis, distance):
    devices = range(lax.axis_size(axis))
    route = [((i - distance) % len(devices), i) for i in devices]
    return lax.ppermute(block, axis, route)


def kept_row(degree, azimuth):
    if azimuth == 0:
        return degree
    if azimuth == 1:
        return 6 + degree
    if azimuth == -1:
        return 12 + degree
    if azimuth == 2:
        return 17 + degree
    return 22 + degree


def to_edge_frame(values, wigner):
    kept_rows = [None] * 29
    offset = 0
    for degree in range(7):
        max_order = min(degree, 2)
        span_cols = 2 * degree + 1
        for azimuth in range(-max_order, max_order + 1):
            running = jnp.zeros(values.shape[1:], jnp.float32)
            for column in range(span_cols):
                factor = wigner[offset + (azimuth + max_order) * span_cols + column].astype(
                    jnp.float32
                )
                running = running + factor[None, :] * values[degree * degree + column].astype(
                    jnp.float32
                )
            kept_rows[kept_row(degree, azimuth)] = running
        offset += (2 * max_order + 1) * span_cols
    return jnp.stack(kept_rows)


def from_edge_frame(kept_rows, wigner):
    full_rows = []
    offset = 0
    for degree in range(7):
        max_order = min(degree, 2)
        span_cols = 2 * degree + 1
        for column in range(span_cols):
            running = jnp.zeros(kept_rows.shape[1:], jnp.float32)
            for azimuth in range(-max_order, max_order + 1):
                factor = wigner[offset + (azimuth + max_order) * span_cols + column].astype(
                    jnp.float32
                )
                running = running + factor[None, :] * kept_rows[kept_row(degree, azimuth)]
            full_rows.append(running)
        offset += (2 * max_order + 1) * span_cols
    return jnp.stack(full_rows)


def contract(weights, grads):
    return lax.dot_general(
        weights, grads, (((2, 3), (0, 1)), ((), ())), preferred_element_type=jnp.float32
    )


def outer(inputs, grads):
    return lax.dot_general(
        inputs, grads, (((2,), (2,)), ((), ())), preferred_element_type=jnp.float32
    )


def so2_back(w_zero, w_one, w_two, edge_grad, edge_in):
    back_rows = [contract(w_zero, edge_grad[0:7])]
    term_zero = outer(edge_in[0:7], edge_grad[0:7])
    weight_terms = []
    for weights, bottom, middle, ceiling in ((w_one, 7, 13, 19), (w_two, 19, 24, 29)):
        grad_plus = edge_grad[bottom:middle]
        grad_minus = edge_grad[middle:ceiling]
        in_plus = edge_in[bottom:middle]
        in_minus = edge_in[middle:ceiling]
        back_rows.append(contract(weights[0], grad_plus) + contract(weights[1], grad_minus))
        back_rows.append(contract(weights[0], grad_minus) - contract(weights[1], grad_plus))
        weight_terms.append(
            jnp.stack(
                [
                    outer(in_plus, grad_plus) + outer(in_minus, grad_minus),
                    outer(in_plus, grad_minus) - outer(in_minus, grad_plus),
                ]
            )
        )
    return (jnp.concatenate(back_rows, axis=0), term_zero, weight_terms[0], weight_terms[1])


def add_columns(summed, term, first_col, axis_dim):
    current = lax.dynamic_slice_in_dim(summed, first_col, term.shape[axis_dim], axis_dim)
    return lax.dynamic_update_slice_in_dim(summed, current + term, first_col, axis_dim)


def body(
    node_x, cotangent, wigner, src_index, dst_index, edge_scale, edge_count, w_zero, w_one, w_two
):
    atom_count = node_x.shape[2]
    own_chan = node_x.shape[1]
    coef_count = node_x.shape[0]
    chan_total = w_zero.shape[3]
    rim_len = atom_count // 4
    slot_count = src_index.shape[0]
    block_len = min(512, slot_count)
    live_count = edge_count[0]
    padded_len = atom_count + 2 * rim_len
    extended = padded(node_x, (("brick", 2),), rim_len)
    at_source = jnp.take(extended, src_index, axis=2)
    edge_in = to_edge_frame(at_source, wigner).astype(jnp.bfloat16)
    block_total = slot_count // block_len
    initial = (
        jnp.zeros((29, own_chan, slot_count), jnp.float32),
        jnp.zeros(w_zero.shape[:3] + (chan_total,), jnp.float32),
        jnp.zeros(w_one.shape[:4] + (chan_total,), jnp.float32),
        jnp.zeros(w_two.shape[:4] + (chan_total,), jnp.float32),
    )
    full_grad = lax.all_gather(cotangent, "chan", axis=1, tiled=True)

    def block_step(block_index, running):
        edge_back, sum_zero, sum_one, sum_two = running
        begin_at = block_index * block_len
        dst_block = lax.dynamic_slice_in_dim(dst_index, begin_at, block_len)
        wig_block = lax.dynamic_slice_in_dim(wigner, begin_at, block_len, 1)
        scale_block = lax.dynamic_slice_in_dim(edge_scale, begin_at, block_len)
        position = begin_at + lax.iota(jnp.int32, block_len)
        factor = jnp.where(position < live_count, 0.25 * scale_block, 0.0)
        at_dest = jnp.take(full_grad, dst_block, axis=2)
        edge_grad = (to_edge_frame(at_dest, wig_block) * factor).astype(jnp.bfloat16)
        edge_block = lax.dynamic_slice_in_dim(edge_in, begin_at, block_len, 2)
        back_rows, term_zero, term_one, term_two = so2_back(
            w_zero, w_one, w_two, edge_grad, edge_block
        )
        edge_back = add_columns(edge_back, back_rows, begin_at, 2)
        sum_zero = add_columns(sum_zero, term_zero, 0, 3)
        sum_one = add_columns(sum_one, term_one, 0, 4)
        sum_two = add_columns(sum_two, term_two, 0, 4)
        return (edge_back, sum_zero, sum_one, sum_two)

    folded = lax.fori_loop(0, block_total, block_step, initial)
    edge_back, sum_zero, sum_one, sum_two = folded

    def back_step(block_index, summed):
        begin_at = block_index * block_len
        kept_rows = lax.dynamic_slice_in_dim(edge_back, begin_at, block_len, 2)
        wig_block = lax.dynamic_slice_in_dim(wigner, begin_at, block_len, 1)
        src_block = lax.dynamic_slice_in_dim(src_index, begin_at, block_len)
        full_rows = from_edge_frame(kept_rows, wig_block)
        onehot = (src_block[:, None] == lax.iota(jnp.int32, padded_len)[None, :]).astype(
            jnp.bfloat16
        )
        high_part = full_rows.astype(jnp.bfloat16)
        rest = full_rows - high_part.astype(jnp.float32)
        low_part = rest.astype(jnp.bfloat16)
        dims = (((2,), (0,)), ((), ()))
        summed = summed + lax.dot_general(
            high_part, onehot, dims, preferred_element_type=jnp.float32
        )
        return summed + lax.dot_general(low_part, onehot, dims, preferred_element_type=jnp.float32)

    grad_ext = lax.fori_loop(
        0, block_total, back_step, jnp.zeros((coef_count, own_chan, padded_len), jnp.float32)
    )
    own_part = grad_ext[:, :, rim_len : rim_len + atom_count]
    from_above = passed_along(grad_ext[:, :, :rim_len], "brick", -1)
    from_below = passed_along(grad_ext[:, :, rim_len + atom_count :], "brick", 1)
    own_part = own_part.at[:, :, :rim_len].add(from_below)
    grad_x = own_part.at[:, :, atom_count - rim_len :].add(from_above)
    return (
        grad_x,
        lax.psum_scatter(sum_zero, "brick", scatter_dimension=3, tiled=True),
        lax.psum_scatter(
            sum_one.reshape((-1,) + sum_one.shape[2:]), "brick", scatter_dimension=3, tiled=True
        ).reshape(sum_one.shape[:4] + (-1,)),
        lax.psum_scatter(
            sum_two.reshape((-1,) + sum_two.shape[2:]), "brick", scatter_dimension=3, tiled=True
        ).reshape(sum_two.shape[:4] + (-1,)),
    )


def solution(mesh):
    in_specs = (
        P(None, "chan", "brick"),
        P(None, "chan", "brick"),
        P(None, "brick"),
        P("brick"),
        P("brick"),
        P("brick"),
        P("brick"),
        P(None, "chan", None, None),
        P(None, None, "chan", None, None),
        P(None, None, "chan", None, None),
    )
    out_specs = (
        P(None, "chan", "brick"),
        P(None, "chan", None, "brick"),
        P(None, None, "chan", None, "brick"),
        P(None, None, "chan", None, "brick"),
    )
    bricks = mesh.shape["brick"]
    fits = bricks % 2 == 0 and bricks > 2 and (128 // bricks) % 16 == 0
    chosen = kernel_body if fits else body
    return jax.shard_map(chosen, mesh=mesh, in_specs=in_specs, out_specs=out_specs, check_vma=False)
```

```python
import functools

import jax
import jax.numpy as jnp
from jax import lax
from jax.experimental import pallas as pl
from jax.experimental.pallas import tpu as pltpu
from jax.sharding import PartitionSpec as P

LANES = 128
VMEM_BYTES = 48 * 1024 * 1024
MESH = pl.DeviceIdType.MESH
NT = (((1,), (1,)), ((), ()))
NN = (((1,), (0,)), ((), ()))


def degree_offset(degree):
    return sum((2 * min(k, 2) + 1) * (2 * k + 1) for k in range(degree))


def rotate_tile(load, wig, store):
    for degree in range(7):
        top = min(degree, 2)
        span = 2 * degree + 1
        offset = degree_offset(degree)
        sums = [None] * (2 * top + 1)
        for column in range(span):
            value = load(degree * degree + column)
            for m in range(2 * top + 1):
                term = wig(offset + m * span + column) * value
                sums[m] = term if sums[m] is None else sums[m] + term
        for m in range(2 * top + 1):
            store(kept_row(degree, m - top), sums[m])


def unrotate_tile(load, wig, store):
    for degree in range(7):
        top = min(degree, 2)
        span = 2 * degree + 1
        offset = degree_offset(degree)
        rows = [load(kept_row(degree, m - top)) for m in range(2 * top + 1)]
        for column in range(span):
            total = None
            for m in range(2 * top + 1):
                term = wig(offset + m * span + column) * rows[m]
                total = term if total is None else total + term
            store(degree * degree + column, total)


def source_onehot(src, rows, rim):
    place = jnp.where(src < rim, src + (rows - rim), src - rim)
    return (lax.broadcasted_iota(jnp.int32, (rows, src.shape[1]), 0) == place).astype(jnp.bfloat16)


def dot(a, b, dims):
    return lax.dot_general(a, b, dims, preferred_element_type=jnp.float32)


def fused_kernel(
    bricks, shards, chan, total, piece, rim, width,
    count_ref, src_ref, dst_ref, scale_ref, wig_ref, cot_ref, x_ref, wz_ref, w1_ref, w2_ref,
    sum_ref, gx_ref,
    wide, scaled, at_dst, at_src, cot, x_next, x_prev, ext, gathered, grad, edge_in,
    wz, w1, w2, back, full, gx, part, near, far, outgoing, to_next, to_prev, from_next, from_prev,
    send_up, send_down, recv_cot, send_x, recv_x, send1, recv1, send2, recv2, send_rim, recv_rim,
):
    me = lax.axis_index("brick")
    z = lax.axis_index("chan")
    core = lax.rem(me, 2)
    mine = lax.div(me, 2)
    pairs = bricks // 2
    sibling = me + 1 - 2 * core
    following = lax.rem(me + 1, bricks)
    previous = lax.rem(me + bricks - 1, bricks)
    atoms = x_ref.shape[1]
    slots = src_ref.shape[1]
    coef = x_ref.shape[0] // chan
    f32, bf16 = jnp.float32, jnp.bfloat16

    barrier = pltpu.get_barrier_semaphore()
    for d in range(1, bricks):
        pl.semaphore_signal(
            barrier, inc=1, device_id={"brick": lax.rem(me + d, bricks)}, device_id_type=MESH
        )

    @pl.when(z > 0)
    def _():
        pl.semaphore_signal(barrier, inc=1, device_id={"chan": z - 1}, device_id_type=MESH)

    @pl.when(z < shards - 1)
    def _():
        pl.semaphore_signal(barrier, inc=1, device_id={"chan": z + 1}, device_id_type=MESH)

    ends = jnp.where(z > 0, 1, 0) + jnp.where(z < shards - 1, 1, 0)
    pl.semaphore_wait(barrier, bricks - 1 + ends)

    def remote(src, dst, send, recv, axis, to):
        return pltpu.make_async_remote_copy(
            src_ref=src, dst_ref=dst, send_sem=send, recv_sem=recv,
            device_id={axis: to}, device_id_type=MESH,
        )

    def up(s, src=None):
        src = cot.at[s] if src is None else src
        return remote(src, cot.at[s], send_up.at[s], recv_cot.at[s], "chan", z + 1)

    def down(s, src=None):
        src = cot.at[s] if src is None else src
        return remote(src, cot.at[s], send_down.at[s], recv_cot.at[s], "chan", z - 1)

    @pl.when(z < shards - 1)
    def _():
        up(z, cot_ref).start()

    @pl.when(z > 0)
    def _():
        down(z, cot_ref).start()

    halos = [
        remote(x_ref, x_next, send_x.at[0], recv_x.at[0], "brick", previous),
        remote(x_ref, x_prev, send_x.at[1], recv_x.at[1], "brick", following),
    ]
    for copy in halos:
        copy.start()

    cot[z] = cot_ref[...]
    position = lax.broadcasted_iota(jnp.int32, (1, slots), 1)
    factor = jnp.where(position < count_ref[0], 0.25 * scale_ref[...], 0.0)
    wide[...] = wig_ref[...].astype(f32)
    scaled[...] = wide[...] * factor
    at_dst[...] = (
        lax.broadcasted_iota(jnp.int32, (atoms, slots), 0) == dst_ref[...]
    ).astype(bf16)
    at_src[...] = source_onehot(src_ref[...], 2 * atoms, rim)
    for kept, source, high in (
        (wz, wz_ref, 7), (w1.at[0], w1_ref.at[0], 6), (w1.at[1], w1_ref.at[1], 6),
        (w2.at[0], w2_ref.at[0], 5), (w2.at[1], w2_ref.at[1], 5),
    ):
        for i in range(high):
            for j in range(high):
                kept[i * chan : (i + 1) * chan, j * total : (j + 1) * total] = source[i, j]

    def rotate_all(values, onehot, entries, out, stride, first):
        def block_step(i, carry):
            cols = pl.ds(pl.multiple_of(i * width, width), width)
            gathered[...] = dot(values(), onehot[:, cols], NN)

            def lanes_step(t, inner):
                near_at = pl.ds(pl.multiple_of(t * LANES, LANES), LANES)
                at = pl.ds(pl.multiple_of(i * width + t * LANES, LANES), LANES)

                def store(row, tile):
                    out[pl.ds(pl.multiple_of(row * stride + first, chan), chan), at] = tile.astype(
                        bf16
                    )

                rotate_tile(
                    lambda c: gathered[c * chan : (c + 1) * chan, near_at],
                    lambda k: entries[k : k + 1, at],
                    store,
                )
                return inner

            lax.fori_loop(0, width // LANES, lanes_step, 0)
            return carry

        lax.fori_loop(0, slots // width, block_step, 0)

    lane = lax.broadcasted_iota(jnp.int32, (1, atoms), 1)

    def distance_step(d, carry):
        low, high = z - d, z + d

        @pl.when((d > 0) & (low >= 0))
        def _():
            down_in = remote(cot_ref, cot.at[low], send_up.at[low], recv_cot.at[low], "chan", z)
            down_in.wait_recv()

            @pl.when(z < shards - 1)
            def _():
                up(low).start()

        @pl.when((d > 0) & (high < shards))
        def _():
            up_in = remote(cot_ref, cot.at[high], send_up.at[high], recv_cot.at[high], "chan", z)
            up_in.wait_recv()

            @pl.when(z > 0)
            def _():
                down(high).start()

        def side_step(side, inner):
            s = jnp.where(side == 0, low, high)

            @pl.when((s >= 0) & (s < shards) & (d + (1 - side) > 0))
            def _():
                rotate_all(lambda: cot[s], at_dst, scaled, grad, total, s * chan)

            return inner

        lax.fori_loop(0, 2, side_step, 0)

        @pl.when(d == 0)
        def _():
            for copy in halos:
                copy.wait_recv()
            ext[:, :atoms] = x_ref[...]
            ext[:, atoms:] = jnp.where(
                lane < rim, x_next[...].astype(f32), x_prev[...].astype(f32)
            ).astype(bf16)
            rotate_all(lambda: ext[...], at_src, wide, edge_in, chan, 0)

        return carry

    lax.fori_loop(0, shards, distance_step, 0)

    def split(row, high, value):
        for c in range(bricks):
            for j in range(high):
                lines = value[j * total + c * piece : j * total + (c + 1) * piece]
                part[c, row + j * piece : row + (j + 1) * piece, : high * chan] = lines.astype(bf16)

    part[...] = jnp.zeros_like(part)
    split(0, 7, dot(grad[: 7 * total], edge_in[: 7 * chan], NT))
    row = 7 * piece
    for first, high in ((7, 6), (19, 5)):
        grad_plus = grad[first * total : (first + high) * total]
        grad_minus = grad[(first + high) * total : (first + 2 * high) * total]
        in_plus = edge_in[first * chan : (first + high) * chan]
        in_minus = edge_in[(first + high) * chan : (first + 2 * high) * chan]
        split(row, high, dot(grad_plus, in_plus, NT) + dot(grad_minus, in_minus, NT))
        row += high * piece
        split(row, high, dot(grad_minus, in_plus, NT) - dot(grad_plus, in_minus, NT))
        row += high * piece

    order = [d for d in range(pairs - 1, 0, -1)] + [0]
    stage_one = []
    for d in order:
        q = lax.rem(mine + d, pairs)
        copy = remote(
            part.at[2 * q + (1 - core)], near.at[d], send1.at[d], recv1.at[d], "brick", sibling
        )
        copy.start()
        stage_one.append(copy)

    gx[...] = jnp.zeros_like(gx)

    def back_block(i, carry):
        cols = pl.ds(pl.multiple_of(i * width, width), width)
        back[: 7 * chan] = dot(wz[...], grad[: 7 * total, cols], NN)
        for w, first, high in ((w1, 7, 6), (w2, 19, 5)):
            low, middle, top = first, first + high, first + 2 * high
            plus = grad[low * total : middle * total, cols]
            minus = grad[middle * total : top * total, cols]
            back[low * chan : middle * chan] = dot(w[0], plus, NN) + dot(w[1], minus, NN)
            back[middle * chan : top * chan] = dot(w[0], minus, NN) - dot(w[1], plus, NN)

        def lanes_step(t, inner):
            near_at = pl.ds(pl.multiple_of(t * LANES, LANES), LANES)
            at = pl.ds(pl.multiple_of(i * width + t * LANES, LANES), LANES)

            def store(c, tile):
                full[c * chan : (c + 1) * chan, near_at] = tile.astype(bf16)

            unrotate_tile(
                lambda r: back[r * chan : (r + 1) * chan, near_at],
                lambda k: wide[k : k + 1, at],
                store,
            )
            return inner

        lax.fori_loop(0, width // LANES, lanes_step, 0)
        gx[: coef * chan] += dot(full[...], at_src[:, cols], NT)
        return carry

    lax.fori_loop(0, 1, back_block, 0)
    stage_two = []
    for copy, d in zip(stage_one, order):
        copy.wait_recv()
        q = lax.rem(mine + d, pairs)
        both = part[2 * q + core].astype(f32) + near[d].astype(f32)
        if d:
            outgoing[d] = both.astype(bf16)
            copy = remote(
                outgoing.at[d], far.at[d], send2.at[d], recv2.at[d], "brick", 2 * q + core
            )
            copy.start()
            stage_two.append(copy)
        else:
            sum_ref[...] = both
    lax.fori_loop(1, slots // width, back_block, 0)

    groups = atoms // rim
    rows = chan // groups
    tile = gx[:, atoms:].reshape(coef + 1, chan, atoms)
    for packed, start in ((to_next, 0), (to_prev, atoms - rim)):
        laid = jnp.zeros((coef + 1, rows, atoms), f32)
        for q in range(groups):
            turn = (q * rim - start) % atoms
            lines = tile[:, q * rows : (q + 1) * rows].reshape(-1, atoms)
            lines = pltpu.roll(lines, turn, 1) if turn else lines
            inside = (lane >= q * rim) & (lane < (q + 1) * rim)
            laid = jnp.where(inside[None], lines.reshape(laid.shape), laid)
        packed[...] = laid.reshape(packed.shape).astype(bf16)
    rims = [
        remote(to_next, from_prev, send_rim.at[0], recv_rim.at[0], "brick", following),
        remote(to_prev, from_next, send_rim.at[1], recv_rim.at[1], "brick", previous),
    ]
    for copy in rims:
        copy.start()
    for copy, d in zip(stage_two, order):
        copy.wait_recv()
        sum_ref[...] += far[d].astype(f32)
    for copy in rims:
        copy.wait_recv()
    arrived = [from_prev[...].astype(f32), from_next[...].astype(f32)]
    for q in range(groups):
        total_lines = gx[: coef * chan, :atoms].reshape(coef, chan, atoms)[
            :, q * rows : (q + 1) * rows
        ]
        for lines, start in zip(arrived, (0, atoms - rim)):
            turn = (start - q * rim) % atoms
            lines = pltpu.roll(lines, turn, 1) if turn else lines
            inside = (lane >= start) & (lane < start + rim)
            lines = jnp.where(inside, lines, 0.0)
            total_lines = total_lines + lines.reshape(coef + 1, rows, atoms)[:coef]
        gx_ref[:, q * rows : (q + 1) * rows, :] = total_lines

    for copy in halos + stage_one + stage_two + rims:
        copy.wait_send()
    for s in range(shards):
        @pl.when((z < shards - 1) & (s <= z))
        def _():
            up(s).wait_send()

        @pl.when((z > 0) & (s >= z))
        def _():
            down(s).wait_send()


def kernel_body(
    node_x, cotangent, wigner, src_index, dst_index, edge_scale, edge_count, w_zero, w_one, w_two
):
    bricks, shards = lax.axis_size("brick"), lax.axis_size("chan")
    coef, chan, atoms = node_x.shape
    total = w_zero.shape[3]
    piece = total // bricks
    rim = atoms // 4
    slots = src_index.shape[0]
    entries = wigner.shape[0]
    width = 256
    f32, bf16 = jnp.float32, jnp.bfloat16
    pairs = bricks // 2
    rows = (7 + 12 + 10) * piece
    flat = coef * chan
    packed = (coef + 1) * (chan * rim // atoms)

    def vmem(shape, dtype):
        return pltpu.VMEM(shape, dtype)

    def dma(count):
        return pltpu.SemaphoreType.DMA((count,))

    whole = pl.BlockSpec(memory_space=pltpu.VMEM)
    sums, grad_x = pl.pallas_call(
        functools.partial(fused_kernel, bricks, shards, chan, total, piece, rim, width),
        out_shape=(
            jax.ShapeDtypeStruct((rows, 2 * LANES), f32),
            jax.ShapeDtypeStruct((coef, chan, atoms), f32),
        ),
        in_specs=[pl.BlockSpec(memory_space=pltpu.SMEM)] + [whole] * 9,
        out_specs=(whole, whole),
        scratch_shapes=[
            vmem((entries, slots), f32), vmem((entries, slots), f32),
            vmem((atoms, slots), bf16), vmem((2 * atoms, slots), bf16),
            vmem((shards, flat, atoms), bf16), vmem((flat, atoms), bf16),
            vmem((flat, atoms), bf16), vmem((flat, 2 * atoms), bf16),
            vmem((flat, width), f32), vmem((29 * total, slots), bf16),
            vmem((29 * chan, slots), bf16), vmem((7 * chan, 7 * total), bf16),
            vmem((2, 6 * chan, 6 * total), bf16), vmem((2, 5 * chan, 5 * total), bf16),
            vmem((29 * chan, width), f32), vmem((flat, width), bf16),
            vmem((flat + chan, 2 * atoms), f32), vmem((bricks, rows, 2 * LANES), bf16),
            vmem((pairs, rows, 2 * LANES), bf16), vmem((pairs, rows, 2 * LANES), bf16),
            vmem((pairs, rows, 2 * LANES), bf16),
            vmem((packed, atoms), bf16), vmem((packed, atoms), bf16),
            vmem((packed, atoms), bf16), vmem((packed, atoms), bf16),
            dma(shards), dma(shards), dma(shards), dma(2), dma(2),
            dma(pairs), dma(pairs), dma(pairs), dma(pairs), dma(2), dma(2),
        ],
        compiler_params=pltpu.CompilerParams(
            vmem_limit_bytes=VMEM_BYTES, collective_id=0, has_side_effects=True
        ),
        name="fused",
    )(
        edge_count, src_index.reshape(1, slots), dst_index.reshape(1, slots),
        edge_scale.reshape(1, slots), wigner, cotangent.reshape(flat, atoms),
        node_x.reshape(flat, atoms), w_zero.transpose(0, 2, 1, 3),
        w_one.transpose(0, 1, 3, 2, 4), w_two.transpose(0, 1, 3, 2, 4),
    )

    def columns_back(first, high):
        block = sums[first : first + high * piece, : high * chan]
        return block.reshape(high, piece, high, chan).transpose(2, 3, 0, 1)

    ends = [0, 7 * piece, 13 * piece, 19 * piece, 24 * piece]
    return (
        grad_x,
        columns_back(ends[0], 7),
        jnp.stack([columns_back(ends[1], 6), columns_back(ends[2], 6)]),
        jnp.stack([columns_back(ends[3], 5), columns_back(ends[4], 5)]),
    )


def padded(x, sides, width):
    for axis, dim in sides:
        devices, length = (lax.axis_size(axis), x.shape[dim])
        up = [(i, (i + 1) % devices) for i in range(devices)]
        down = [(j, i) for i, j in up]
        last = lax.slice_in_dim(x, length - width, length, axis=dim)
        initial = lax.slice_in_dim(x, 0, width, axis=dim)
        before = lax.ppermute(last, axis, up)
        after = lax.ppermute(initial, axis, down)
        x = jnp.concatenate([before, x, after], axis=dim)
    return x


def passed_along(block, axis, distance):
    devices = range(lax.axis_size(axis))
    route = [((i - distance) % len(devices), i) for i in devices]
    return lax.ppermute(block, axis, route)


def kept_row(degree, azimuth):
    if azimuth == 0:
        return degree
    if azimuth == 1:
        return 6 + degree
    if azimuth == -1:
        return 12 + degree
    if azimuth == 2:
        return 17 + degree
    return 22 + degree


def to_edge_frame(values, wigner):
    kept_rows = [None] * 29
    offset = 0
    for degree in range(7):
        max_order = min(degree, 2)
        span_cols = 2 * degree + 1
        for azimuth in range(-max_order, max_order + 1):
            running = jnp.zeros(values.shape[1:], jnp.float32)
            for column in range(span_cols):
                factor = wigner[offset + (azimuth + max_order) * span_cols + column].astype(
                    jnp.float32
                )
                running = running + factor[None, :] * values[degree * degree + column].astype(
                    jnp.float32
                )
            kept_rows[kept_row(degree, azimuth)] = running
        offset += (2 * max_order + 1) * span_cols
    return jnp.stack(kept_rows)


def from_edge_frame(kept_rows, wigner):
    full_rows = []
    offset = 0
    for degree in range(7):
        max_order = min(degree, 2)
        span_cols = 2 * degree + 1
        for column in range(span_cols):
            running = jnp.zeros(kept_rows.shape[1:], jnp.float32)
            for azimuth in range(-max_order, max_order + 1):
                factor = wigner[offset + (azimuth + max_order) * span_cols + column].astype(
                    jnp.float32
                )
                running = running + factor[None, :] * kept_rows[kept_row(degree, azimuth)]
            full_rows.append(running)
        offset += (2 * max_order + 1) * span_cols
    return jnp.stack(full_rows)


def contract(weights, grads):
    return lax.dot_general(
        weights, grads, (((2, 3), (0, 1)), ((), ())), preferred_element_type=jnp.float32
    )


def outer(inputs, grads):
    return lax.dot_general(
        inputs, grads, (((2,), (2,)), ((), ())), preferred_element_type=jnp.float32
    )


def so2_back(w_zero, w_one, w_two, edge_grad, edge_in):
    back_rows = [contract(w_zero, edge_grad[0:7])]
    term_zero = outer(edge_in[0:7], edge_grad[0:7])
    weight_terms = []
    for weights, bottom, middle, ceiling in ((w_one, 7, 13, 19), (w_two, 19, 24, 29)):
        grad_plus = edge_grad[bottom:middle]
        grad_minus = edge_grad[middle:ceiling]
        in_plus = edge_in[bottom:middle]
        in_minus = edge_in[middle:ceiling]
        back_rows.append(contract(weights[0], grad_plus) + contract(weights[1], grad_minus))
        back_rows.append(contract(weights[0], grad_minus) - contract(weights[1], grad_plus))
        weight_terms.append(
            jnp.stack(
                [
                    outer(in_plus, grad_plus) + outer(in_minus, grad_minus),
                    outer(in_plus, grad_minus) - outer(in_minus, grad_plus),
                ]
            )
        )
    return (jnp.concatenate(back_rows, axis=0), term_zero, weight_terms[0], weight_terms[1])


def add_columns(summed, term, first_col, axis_dim):
    current = lax.dynamic_slice_in_dim(summed, first_col, term.shape[axis_dim], axis_dim)
    return lax.dynamic_update_slice_in_dim(summed, current + term, first_col, axis_dim)


def body(
    node_x, cotangent, wigner, src_index, dst_index, edge_scale, edge_count, w_zero, w_one, w_two
):
    atom_count = node_x.shape[2]
    own_chan = node_x.shape[1]
    coef_count = node_x.shape[0]
    chan_total = w_zero.shape[3]
    rim_len = atom_count // 4
    slot_count = src_index.shape[0]
    block_len = min(512, slot_count)
    live_count = edge_count[0]
    padded_len = atom_count + 2 * rim_len
    extended = padded(node_x, (("brick", 2),), rim_len)
    at_source = jnp.take(extended, src_index, axis=2)
    edge_in = to_edge_frame(at_source, wigner).astype(jnp.bfloat16)
    block_total = slot_count // block_len
    initial = (
        jnp.zeros((29, own_chan, slot_count), jnp.float32),
        jnp.zeros(w_zero.shape[:3] + (chan_total,), jnp.float32),
        jnp.zeros(w_one.shape[:4] + (chan_total,), jnp.float32),
        jnp.zeros(w_two.shape[:4] + (chan_total,), jnp.float32),
    )
    full_grad = lax.all_gather(cotangent, "chan", axis=1, tiled=True)

    def block_step(block_index, running):
        edge_back, sum_zero, sum_one, sum_two = running
        begin_at = block_index * block_len
        dst_block = lax.dynamic_slice_in_dim(dst_index, begin_at, block_len)
        wig_block = lax.dynamic_slice_in_dim(wigner, begin_at, block_len, 1)
        scale_block = lax.dynamic_slice_in_dim(edge_scale, begin_at, block_len)
        position = begin_at + lax.iota(jnp.int32, block_len)
        factor = jnp.where(position < live_count, 0.25 * scale_block, 0.0)
        at_dest = jnp.take(full_grad, dst_block, axis=2)
        edge_grad = (to_edge_frame(at_dest, wig_block) * factor).astype(jnp.bfloat16)
        edge_block = lax.dynamic_slice_in_dim(edge_in, begin_at, block_len, 2)
        back_rows, term_zero, term_one, term_two = so2_back(
            w_zero, w_one, w_two, edge_grad, edge_block
        )
        edge_back = add_columns(edge_back, back_rows, begin_at, 2)
        sum_zero = add_columns(sum_zero, term_zero, 0, 3)
        sum_one = add_columns(sum_one, term_one, 0, 4)
        sum_two = add_columns(sum_two, term_two, 0, 4)
        return (edge_back, sum_zero, sum_one, sum_two)

    folded = lax.fori_loop(0, block_total, block_step, initial)
    edge_back, sum_zero, sum_one, sum_two = folded

    def back_step(block_index, summed):
        begin_at = block_index * block_len
        kept_rows = lax.dynamic_slice_in_dim(edge_back, begin_at, block_len, 2)
        wig_block = lax.dynamic_slice_in_dim(wigner, begin_at, block_len, 1)
        src_block = lax.dynamic_slice_in_dim(src_index, begin_at, block_len)
        full_rows = from_edge_frame(kept_rows, wig_block)
        onehot = (src_block[:, None] == lax.iota(jnp.int32, padded_len)[None, :]).astype(
            jnp.bfloat16
        )
        high_part = full_rows.astype(jnp.bfloat16)
        rest = full_rows - high_part.astype(jnp.float32)
        low_part = rest.astype(jnp.bfloat16)
        dims = (((2,), (0,)), ((), ()))
        summed = summed + lax.dot_general(
            high_part, onehot, dims, preferred_element_type=jnp.float32
        )
        return summed + lax.dot_general(low_part, onehot, dims, preferred_element_type=jnp.float32)

    grad_ext = lax.fori_loop(
        0, block_total, back_step, jnp.zeros((coef_count, own_chan, padded_len), jnp.float32)
    )
    own_part = grad_ext[:, :, rim_len : rim_len + atom_count]
    from_above = passed_along(grad_ext[:, :, :rim_len], "brick", -1)
    from_below = passed_along(grad_ext[:, :, rim_len + atom_count :], "brick", 1)
    own_part = own_part.at[:, :, :rim_len].add(from_below)
    grad_x = own_part.at[:, :, atom_count - rim_len :].add(from_above)
    return (
        grad_x,
        lax.psum_scatter(sum_zero, "brick", scatter_dimension=3, tiled=True),
        lax.psum_scatter(
            sum_one.reshape((-1,) + sum_one.shape[2:]), "brick", scatter_dimension=3, tiled=True
        ).reshape(sum_one.shape[:4] + (-1,)),
        lax.psum_scatter(
            sum_two.reshape((-1,) + sum_two.shape[2:]), "brick", scatter_dimension=3, tiled=True
        ).reshape(sum_two.shape[:4] + (-1,)),
    )


def solution(mesh):
    in_specs = (
        P(None, "chan", "brick"),
        P(None, "chan", "brick"),
        P(None, "brick"),
        P("brick"),
        P("brick"),
        P("brick"),
        P("brick"),
        P(None, "chan", None, None),
        P(None, None, "chan", None, None),
        P(None, None, "chan", None, None),
    )
    out_specs = (
        P(None, "chan", "brick"),
        P(None, "chan", None, "brick"),
        P(None, None, "chan", None, "brick"),
        P(None, None, "chan", None, "brick"),
    )
    bricks, shards = mesh.shape["brick"], mesh.shape["chan"]
    fits = bricks % 2 == 0 and bricks > 2 and (128 // bricks) % 16 == 0 and shards <= 4
    chosen = kernel_body if fits else body
    return jax.shard_map(chosen, mesh=mesh, in_specs=in_specs, out_specs=out_specs, check_vma=False)
```

```python
import functools

import jax
import jax.numpy as jnp
from jax import lax
from jax.experimental import pallas as pl
from jax.experimental.pallas import tpu as pltpu
from jax.sharding import PartitionSpec as P

LANES = 128
VMEM_BYTES = 48 * 1024 * 1024
MESH = pl.DeviceIdType.MESH
NT = (((1,), (1,)), ((), ()))
NN = (((1,), (0,)), ((), ()))


def degree_offset(degree):
    return sum((2 * min(k, 2) + 1) * (2 * k + 1) for k in range(degree))


def rotate_tile(load, wig, store):
    for degree in range(7):
        top = min(degree, 2)
        span = 2 * degree + 1
        offset = degree_offset(degree)
        sums = [None] * (2 * top + 1)
        for column in range(span):
            value = load(degree * degree + column)
            for m in range(2 * top + 1):
                term = wig(offset + m * span + column) * value
                sums[m] = term if sums[m] is None else sums[m] + term
        for m in range(2 * top + 1):
            store(kept_row(degree, m - top), sums[m])


def unrotate_tile(load, wig, store):
    for degree in range(7):
        top = min(degree, 2)
        span = 2 * degree + 1
        offset = degree_offset(degree)
        rows = [load(kept_row(degree, m - top)) for m in range(2 * top + 1)]
        for column in range(span):
            total = None
            for m in range(2 * top + 1):
                term = wig(offset + m * span + column) * rows[m]
                total = term if total is None else total + term
            store(degree * degree + column, total)


def source_onehot(src, rows, rim):
    place = jnp.where(src < rim, src + (rows - rim), src - rim)
    return (lax.broadcasted_iota(jnp.int32, (rows, src.shape[1]), 0) == place).astype(jnp.bfloat16)


def dot(a, b, dims):
    return lax.dot_general(a, b, dims, preferred_element_type=jnp.float32)


def fused_kernel(
    bricks, shards, chan, total, piece, rim, width,
    count_ref, src_ref, dst_ref, scale_ref, wig_ref, cot_ref, x_ref, wz_ref, w1_ref, w2_ref,
    sum_ref, gx_ref,
    wig_in, wz_in, w1_in, w2_in,
    wide, scaled, at_dst, at_src, cot, x_next, x_prev, ext, gathered, grad, edge_in,
    wz, w1, w2, back, full, gx, part, near, far, outgoing, to_next, to_prev, from_next, from_prev,
    local, send_up, send_down, recv_cot, send_x, recv_x, send1, recv1, send2, recv2,
    send_rim, recv_rim,
):
    me = lax.axis_index("brick")
    z = lax.axis_index("chan")
    core = lax.rem(me, 2)
    mine = lax.div(me, 2)
    pairs = bricks // 2
    sibling = me + 1 - 2 * core
    following = lax.rem(me + 1, bricks)
    previous = lax.rem(me + bricks - 1, bricks)
    atoms = x_ref.shape[1]
    slots = src_ref.shape[1]
    copies = [
        pltpu.make_async_copy(source, target, local.at[i])
        for i, (source, target) in enumerate((
            (wig_ref, wig_in), (cot_ref, cot.at[z]), (x_ref, ext.at[:, :atoms]),
            (wz_ref, wz_in), (w1_ref, w1_in), (w2_ref, w2_in),
        ))
    ]
    for copy in copies:
        copy.start()
    coef = x_ref.shape[0] // chan
    f32, bf16 = jnp.float32, jnp.bfloat16

    barrier = pltpu.get_barrier_semaphore()
    for d in range(1, bricks):
        pl.semaphore_signal(
            barrier, inc=1, device_id={"brick": lax.rem(me + d, bricks)}, device_id_type=MESH
        )

    @pl.when(z > 0)
    def _():
        pl.semaphore_signal(barrier, inc=1, device_id={"chan": z - 1}, device_id_type=MESH)

    @pl.when(z < shards - 1)
    def _():
        pl.semaphore_signal(barrier, inc=1, device_id={"chan": z + 1}, device_id_type=MESH)

    ends = jnp.where(z > 0, 1, 0) + jnp.where(z < shards - 1, 1, 0)
    pl.semaphore_wait(barrier, bricks - 1 + ends)

    def remote(src, dst, send, recv, axis, to):
        return pltpu.make_async_remote_copy(
            src_ref=src, dst_ref=dst, send_sem=send, recv_sem=recv,
            device_id={axis: to}, device_id_type=MESH,
        )

    def up(s, src=None):
        src = cot.at[s] if src is None else src
        return remote(src, cot.at[s], send_up.at[s], recv_cot.at[s], "chan", z + 1)

    def down(s, src=None):
        src = cot.at[s] if src is None else src
        return remote(src, cot.at[s], send_down.at[s], recv_cot.at[s], "chan", z - 1)

    @pl.when(z < shards - 1)
    def _():
        up(z, cot_ref).start()

    @pl.when(z > 0)
    def _():
        down(z, cot_ref).start()

    halos = [
        remote(x_ref, x_next, send_x.at[0], recv_x.at[0], "brick", previous),
        remote(x_ref, x_prev, send_x.at[1], recv_x.at[1], "brick", following),
    ]
    for copy in halos:
        copy.start()

    at_dst[...] = (
        lax.broadcasted_iota(jnp.int32, (atoms, slots), 0) == dst_ref[...]
    ).astype(bf16)
    at_src[...] = source_onehot(src_ref[...], 2 * atoms, rim)
    back[...] = jnp.zeros_like(back)
    position = lax.broadcasted_iota(jnp.int32, (1, slots), 1)
    factor = jnp.where(position < count_ref[0], 0.25 * scale_ref[...], 0.0)
    copies[0].wait()
    wide[...] = wig_in[...].astype(f32)
    scaled[...] = wide[...] * factor
    copies[1].wait()

    def rotate_all(values, onehot, entries, out, stride, first):
        def block_step(i, carry):
            cols = pl.ds(pl.multiple_of(i * width, width), width)
            gathered[...] = dot(values(), onehot[:, cols], NN)

            def lanes_step(t, inner):
                near_at = pl.ds(pl.multiple_of(t * LANES, LANES), LANES)
                at = pl.ds(pl.multiple_of(i * width + t * LANES, LANES), LANES)

                def store(row, tile):
                    out[pl.ds(pl.multiple_of(row * stride + first, chan), chan), at] = tile.astype(
                        bf16
                    )

                rotate_tile(
                    lambda c: gathered[c * chan : (c + 1) * chan, near_at],
                    lambda k: entries[k : k + 1, at],
                    store,
                )
                return inner

            lax.fori_loop(0, width // LANES, lanes_step, 0)
            return carry

        lax.fori_loop(0, slots // width, block_step, 0)

    lane = lax.broadcasted_iota(jnp.int32, (1, atoms), 1)

    def first_shard():
        for copy in copies[3:]:
            copy.wait()
        for kept, source, lead, high in (
            (wz, wz_in, (), 7), (w1, w1_in, (0,), 6), (w1, w1_in, (1,), 6),
            (w2, w2_in, (0,), 5), (w2, w2_in, (1,), 5),
        ):
            for i in range(high):
                for j in range(high):
                    tile = source[lead + (i, j)]
                    for s in range(shards):
                        kept[
                            lead + (s, slice(i * chan, (i + 1) * chan),
                                    slice(j * chan, (j + 1) * chan))
                        ] = tile[:, s * chan : (s + 1) * chan]
        copies[2].wait()
        for copy in halos:
            copy.wait_recv()
        ext[:, atoms:] = jnp.where(
            lane < rim, x_next[...].astype(f32), x_prev[...].astype(f32)
        ).astype(bf16)
        rotate_all(lambda: ext[...], at_src, wide, edge_in, chan, 0)
        part[...] = jnp.zeros_like(part)

    def stage_one(s):
        return remote(
            part.at[2 * s + (1 - core)], near.at[s], send1.at[s], recv1.at[s], "brick", sibling
        )

    def stage_two(s, d):
        return remote(
            outgoing.at[s], far.at[d], send2.at[d], recv2.at[d], "brick", 2 * s + core
        )

    def shard_products(s):
        def split(row, high, value):
            for h in range(2):
                for j in range(high):
                    lines = value[j * chan + h * piece : j * chan + (h + 1) * piece]
                    part[2 * s + h, row + j * piece : row + (j + 1) * piece, : high * chan] = (
                        lines.astype(bf16)
                    )

        split(0, 7, dot(grad[: 7 * chan], edge_in[: 7 * chan], NT))
        row = 7 * piece
        for first, high in ((7, 6), (19, 5)):
            low, middle, top = first * chan, (first + high) * chan, (first + 2 * high) * chan
            grad_plus, grad_minus = grad[low:middle], grad[middle:top]
            in_plus, in_minus = edge_in[low:middle], edge_in[middle:top]
            split(row, high, dot(grad_plus, in_plus, NT) + dot(grad_minus, in_minus, NT))
            row += high * piece
            split(row, high, dot(grad_minus, in_plus, NT) - dot(grad_plus, in_minus, NT))
            row += high * piece
        stage_one(s).start()

        def contract_step(i, carry):
            cols = pl.ds(pl.multiple_of(i * width, width), width)
            back[: 7 * chan, cols] += dot(wz[s], grad[: 7 * chan, cols], NN)
            for w, first, high in ((w1, 7, 6), (w2, 19, 5)):
                low, middle, top = first * chan, (first + high) * chan, (first + 2 * high) * chan
                plus, minus = grad[low:middle, cols], grad[middle:top, cols]
                back[low:middle, cols] += dot(w[0, s], plus, NN) + dot(w[1, s], minus, NN)
                back[middle:top, cols] += dot(w[0, s], minus, NN) - dot(w[1, s], plus, NN)
            return carry

        lax.fori_loop(0, slots // width, contract_step, 0)
        stage_one(s).wait_recv()
        both = part[2 * s + core].astype(f32) + near[s].astype(f32)

        @pl.when(s == mine)
        def _():
            sum_ref[...] = both

        @pl.when(s != mine)
        def _():
            outgoing[s] = both.astype(bf16)
            stage_two(s, lax.rem(s - mine + pairs, pairs)).start()

    def distance_step(d, carry):
        low, high = z - d, z + d

        @pl.when((d > 0) & (low >= 0))
        def _():
            down_in = remote(cot_ref, cot.at[low], send_up.at[low], recv_cot.at[low], "chan", z)
            down_in.wait_recv()

            @pl.when(z < shards - 1)
            def _():
                up(low).start()

        @pl.when((d > 0) & (high < shards))
        def _():
            up_in = remote(cot_ref, cot.at[high], send_up.at[high], recv_cot.at[high], "chan", z)
            up_in.wait_recv()

            @pl.when(z > 0)
            def _():
                down(high).start()

        def side_step(side, inner):
            s = jnp.where(side == 0, low, high)

            @pl.when((s >= 0) & (s < shards) & (d + (1 - side) > 0))
            def _():
                rotate_all(lambda: cot[s], at_dst, scaled, grad, chan, 0)

                @pl.when(d == 0)
                def _():
                    first_shard()

                shard_products(s)

            return inner

        lax.fori_loop(0, 2, side_step, 0)
        return carry

    lax.fori_loop(0, shards, distance_step, 0)

    gx[...] = jnp.zeros_like(gx)

    def back_block(i, carry):
        cols = pl.ds(pl.multiple_of(i * width, width), width)

        def lanes_step(t, inner):
            near_at = pl.ds(pl.multiple_of(t * LANES, LANES), LANES)
            at = pl.ds(pl.multiple_of(i * width + t * LANES, LANES), LANES)

            def store(c, tile):
                full[c * chan : (c + 1) * chan, near_at] = tile.astype(bf16)

            unrotate_tile(
                lambda r: back[r * chan : (r + 1) * chan, at],
                lambda k: wide[k : k + 1, at],
                store,
            )
            return inner

        lax.fori_loop(0, width // LANES, lanes_step, 0)
        gx[: coef * chan] += dot(full[...], at_src[:, cols], NT)
        return carry

    lax.fori_loop(0, slots // width, back_block, 0)

    groups = atoms // rim
    rows = chan // groups
    tile = gx[:, atoms:].reshape(coef + 1, chan, atoms)
    for packed, start in ((to_next, 0), (to_prev, atoms - rim)):
        laid = jnp.zeros((coef + 1, rows, atoms), f32)
        for q in range(groups):
            turn = (q * rim - start) % atoms
            lines = tile[:, q * rows : (q + 1) * rows].reshape(-1, atoms)
            lines = pltpu.roll(lines, turn, 1) if turn else lines
            inside = (lane >= q * rim) & (lane < (q + 1) * rim)
            laid = jnp.where(inside[None], lines.reshape(laid.shape), laid)
        packed[...] = laid.reshape(packed.shape).astype(bf16)
    rims = [
        remote(to_next, from_prev, send_rim.at[0], recv_rim.at[0], "brick", following),
        remote(to_prev, from_next, send_rim.at[1], recv_rim.at[1], "brick", previous),
    ]
    for copy in rims:
        copy.start()
    for d in range(1, pairs):
        stage_two(0, d).wait_recv()
        sum_ref[...] += far[d].astype(f32)
    for copy in rims:
        copy.wait_recv()
    arrived = [from_prev[...].astype(f32), from_next[...].astype(f32)]
    for q in range(groups):
        total_lines = gx[: coef * chan, :atoms].reshape(coef, chan, atoms)[
            :, q * rows : (q + 1) * rows
        ]
        for lines, start in zip(arrived, (0, atoms - rim)):
            turn = (start - q * rim) % atoms
            lines = pltpu.roll(lines, turn, 1) if turn else lines
            inside = (lane >= start) & (lane < start + rim)
            lines = jnp.where(inside, lines, 0.0)
            total_lines = total_lines + lines.reshape(coef + 1, rows, atoms)[:coef]
        gx_ref[:, q * rows : (q + 1) * rows, :] = total_lines

    for copy in halos + rims:
        copy.wait_send()
    for d in range(1, pairs):
        stage_two(0, d).wait_send()
    for s in range(shards):
        stage_one(s).wait_send()

        @pl.when((z < shards - 1) & (s <= z))
        def _():
            up(s).wait_send()

        @pl.when((z > 0) & (s >= z))
        def _():
            down(s).wait_send()


def kernel_body(
    node_x, cotangent, wigner, src_index, dst_index, edge_scale, edge_count, w_zero, w_one, w_two
):
    bricks, shards = lax.axis_size("brick"), lax.axis_size("chan")
    coef, chan, atoms = node_x.shape
    total = w_zero.shape[3]
    piece = total // bricks
    rim = atoms // 4
    slots = src_index.shape[0]
    entries = wigner.shape[0]
    width = 256
    f32, bf16 = jnp.float32, jnp.bfloat16
    pairs = bricks // 2
    rows = (7 + 12 + 10) * piece
    flat = coef * chan
    packed = (coef + 1) * (chan * rim // atoms)

    def vmem(shape, dtype):
        return pltpu.VMEM(shape, dtype)

    def dma(count):
        return pltpu.SemaphoreType.DMA((count,))

    whole = pl.BlockSpec(memory_space=pltpu.VMEM)
    hbm = pl.BlockSpec(memory_space=pltpu.HBM)
    sums, grad_x = pl.pallas_call(
        functools.partial(fused_kernel, bricks, shards, chan, total, piece, rim, width),
        out_shape=(
            jax.ShapeDtypeStruct((rows, 2 * LANES), f32),
            jax.ShapeDtypeStruct((coef, chan, atoms), f32),
        ),
        in_specs=[pl.BlockSpec(memory_space=pltpu.SMEM)] + [whole] * 3 + [hbm] * 6,
        out_specs=(whole, whole),
        scratch_shapes=[
            vmem((entries, slots), bf16), vmem((7, 7, chan, total), bf16),
            vmem((2, 6, 6, chan, total), bf16), vmem((2, 5, 5, chan, total), bf16),
            vmem((entries, slots), f32), vmem((entries, slots), f32),
            vmem((atoms, slots), bf16), vmem((2 * atoms, slots), bf16),
            vmem((shards, flat, atoms), bf16), vmem((flat, atoms), bf16),
            vmem((flat, atoms), bf16), vmem((flat, 2 * atoms), bf16),
            vmem((flat, width), f32), vmem((29 * chan, slots), bf16),
            vmem((29 * chan, slots), bf16), vmem((shards, 7 * chan, 7 * chan), bf16),
            vmem((2, shards, 6 * chan, 6 * chan), bf16),
            vmem((2, shards, 5 * chan, 5 * chan), bf16),
            vmem((29 * chan, slots), f32), vmem((flat, width), bf16),
            vmem((flat + chan, 2 * atoms), f32), vmem((bricks, rows, 2 * LANES), bf16),
            vmem((pairs, rows, 2 * LANES), bf16), vmem((pairs, rows, 2 * LANES), bf16),
            vmem((pairs, rows, 2 * LANES), bf16),
            vmem((packed, atoms), bf16), vmem((packed, atoms), bf16),
            vmem((packed, atoms), bf16), vmem((packed, atoms), bf16),
            dma(6), dma(shards), dma(shards), dma(shards), dma(2), dma(2),
            dma(pairs), dma(pairs), dma(pairs), dma(pairs), dma(2), dma(2),
        ],
        compiler_params=pltpu.CompilerParams(
            vmem_limit_bytes=VMEM_BYTES, collective_id=0, has_side_effects=True
        ),
        name="fused",
    )(
        edge_count, src_index.reshape(1, slots), dst_index.reshape(1, slots),
        edge_scale.reshape(1, slots), wigner, cotangent.reshape(flat, atoms),
        node_x.reshape(flat, atoms), w_zero.transpose(0, 2, 1, 3),
        w_one.transpose(0, 1, 3, 2, 4), w_two.transpose(0, 1, 3, 2, 4),
    )

    def columns_back(first, high):
        block = sums[first : first + high * piece, : high * chan]
        return block.reshape(high, piece, high, chan).transpose(2, 3, 0, 1)

    ends = [0, 7 * piece, 13 * piece, 19 * piece, 24 * piece]
    return (
        grad_x,
        columns_back(ends[0], 7),
        jnp.stack([columns_back(ends[1], 6), columns_back(ends[2], 6)]),
        jnp.stack([columns_back(ends[3], 5), columns_back(ends[4], 5)]),
    )


def padded(x, sides, width):
    for axis, dim in sides:
        devices, length = (lax.axis_size(axis), x.shape[dim])
        up = [(i, (i + 1) % devices) for i in range(devices)]
        down = [(j, i) for i, j in up]
        last = lax.slice_in_dim(x, length - width, length, axis=dim)
        initial = lax.slice_in_dim(x, 0, width, axis=dim)
        before = lax.ppermute(last, axis, up)
        after = lax.ppermute(initial, axis, down)
        x = jnp.concatenate([before, x, after], axis=dim)
    return x


def passed_along(block, axis, distance):
    devices = range(lax.axis_size(axis))
    route = [((i - distance) % len(devices), i) for i in devices]
    return lax.ppermute(block, axis, route)


def kept_row(degree, azimuth):
    if azimuth == 0:
        return degree
    if azimuth == 1:
        return 6 + degree
    if azimuth == -1:
        return 12 + degree
    if azimuth == 2:
        return 17 + degree
    return 22 + degree


def to_edge_frame(values, wigner):
    kept_rows = [None] * 29
    offset = 0
    for degree in range(7):
        max_order = min(degree, 2)
        span_cols = 2 * degree + 1
        for azimuth in range(-max_order, max_order + 1):
            running = jnp.zeros(values.shape[1:], jnp.float32)
            for column in range(span_cols):
                factor = wigner[offset + (azimuth + max_order) * span_cols + column].astype(
                    jnp.float32
                )
                running = running + factor[None, :] * values[degree * degree + column].astype(
                    jnp.float32
                )
            kept_rows[kept_row(degree, azimuth)] = running
        offset += (2 * max_order + 1) * span_cols
    return jnp.stack(kept_rows)


def from_edge_frame(kept_rows, wigner):
    full_rows = []
    offset = 0
    for degree in range(7):
        max_order = min(degree, 2)
        span_cols = 2 * degree + 1
        for column in range(span_cols):
            running = jnp.zeros(kept_rows.shape[1:], jnp.float32)
            for azimuth in range(-max_order, max_order + 1):
                factor = wigner[offset + (azimuth + max_order) * span_cols + column].astype(
                    jnp.float32
                )
                running = running + factor[None, :] * kept_rows[kept_row(degree, azimuth)]
            full_rows.append(running)
        offset += (2 * max_order + 1) * span_cols
    return jnp.stack(full_rows)


def contract(weights, grads):
    return lax.dot_general(
        weights, grads, (((2, 3), (0, 1)), ((), ())), preferred_element_type=jnp.float32
    )


def outer(inputs, grads):
    return lax.dot_general(
        inputs, grads, (((2,), (2,)), ((), ())), preferred_element_type=jnp.float32
    )


def so2_back(w_zero, w_one, w_two, edge_grad, edge_in):
    back_rows = [contract(w_zero, edge_grad[0:7])]
    term_zero = outer(edge_in[0:7], edge_grad[0:7])
    weight_terms = []
    for weights, bottom, middle, ceiling in ((w_one, 7, 13, 19), (w_two, 19, 24, 29)):
        grad_plus = edge_grad[bottom:middle]
        grad_minus = edge_grad[middle:ceiling]
        in_plus = edge_in[bottom:middle]
        in_minus = edge_in[middle:ceiling]
        back_rows.append(contract(weights[0], grad_plus) + contract(weights[1], grad_minus))
        back_rows.append(contract(weights[0], grad_minus) - contract(weights[1], grad_plus))
        weight_terms.append(
            jnp.stack(
                [
                    outer(in_plus, grad_plus) + outer(in_minus, grad_minus),
                    outer(in_plus, grad_minus) - outer(in_minus, grad_plus),
                ]
            )
        )
    return (jnp.concatenate(back_rows, axis=0), term_zero, weight_terms[0], weight_terms[1])


def add_columns(summed, term, first_col, axis_dim):
    current = lax.dynamic_slice_in_dim(summed, first_col, term.shape[axis_dim], axis_dim)
    return lax.dynamic_update_slice_in_dim(summed, current + term, first_col, axis_dim)


def body(
    node_x, cotangent, wigner, src_index, dst_index, edge_scale, edge_count, w_zero, w_one, w_two
):
    atom_count = node_x.shape[2]
    own_chan = node_x.shape[1]
    coef_count = node_x.shape[0]
    chan_total = w_zero.shape[3]
    rim_len = atom_count // 4
    slot_count = src_index.shape[0]
    block_len = min(512, slot_count)
    live_count = edge_count[0]
    padded_len = atom_count + 2 * rim_len
    extended = padded(node_x, (("brick", 2),), rim_len)
    at_source = jnp.take(extended, src_index, axis=2)
    edge_in = to_edge_frame(at_source, wigner).astype(jnp.bfloat16)
    block_total = slot_count // block_len
    initial = (
        jnp.zeros((29, own_chan, slot_count), jnp.float32),
        jnp.zeros(w_zero.shape[:3] + (chan_total,), jnp.float32),
        jnp.zeros(w_one.shape[:4] + (chan_total,), jnp.float32),
        jnp.zeros(w_two.shape[:4] + (chan_total,), jnp.float32),
    )
    full_grad = lax.all_gather(cotangent, "chan", axis=1, tiled=True)

    def block_step(block_index, running):
        edge_back, sum_zero, sum_one, sum_two = running
        begin_at = block_index * block_len
        dst_block = lax.dynamic_slice_in_dim(dst_index, begin_at, block_len)
        wig_block = lax.dynamic_slice_in_dim(wigner, begin_at, block_len, 1)
        scale_block = lax.dynamic_slice_in_dim(edge_scale, begin_at, block_len)
        position = begin_at + lax.iota(jnp.int32, block_len)
        factor = jnp.where(position < live_count, 0.25 * scale_block, 0.0)
        at_dest = jnp.take(full_grad, dst_block, axis=2)
        edge_grad = (to_edge_frame(at_dest, wig_block) * factor).astype(jnp.bfloat16)
        edge_block = lax.dynamic_slice_in_dim(edge_in, begin_at, block_len, 2)
        back_rows, term_zero, term_one, term_two = so2_back(
            w_zero, w_one, w_two, edge_grad, edge_block
        )
        edge_back = add_columns(edge_back, back_rows, begin_at, 2)
        sum_zero = add_columns(sum_zero, term_zero, 0, 3)
        sum_one = add_columns(sum_one, term_one, 0, 4)
        sum_two = add_columns(sum_two, term_two, 0, 4)
        return (edge_back, sum_zero, sum_one, sum_two)

    folded = lax.fori_loop(0, block_total, block_step, initial)
    edge_back, sum_zero, sum_one, sum_two = folded

    def back_step(block_index, summed):
        begin_at = block_index * block_len
        kept_rows = lax.dynamic_slice_in_dim(edge_back, begin_at, block_len, 2)
        wig_block = lax.dynamic_slice_in_dim(wigner, begin_at, block_len, 1)
        src_block = lax.dynamic_slice_in_dim(src_index, begin_at, block_len)
        full_rows = from_edge_frame(kept_rows, wig_block)
        onehot = (src_block[:, None] == lax.iota(jnp.int32, padded_len)[None, :]).astype(
            jnp.bfloat16
        )
        high_part = full_rows.astype(jnp.bfloat16)
        rest = full_rows - high_part.astype(jnp.float32)
        low_part = rest.astype(jnp.bfloat16)
        dims = (((2,), (0,)), ((), ()))
        summed = summed + lax.dot_general(
            high_part, onehot, dims, preferred_element_type=jnp.float32
        )
        return summed + lax.dot_general(low_part, onehot, dims, preferred_element_type=jnp.float32)

    grad_ext = lax.fori_loop(
        0, block_total, back_step, jnp.zeros((coef_count, own_chan, padded_len), jnp.float32)
    )
    own_part = grad_ext[:, :, rim_len : rim_len + atom_count]
    from_above = passed_along(grad_ext[:, :, :rim_len], "brick", -1)
    from_below = passed_along(grad_ext[:, :, rim_len + atom_count :], "brick", 1)
    own_part = own_part.at[:, :, :rim_len].add(from_below)
    grad_x = own_part.at[:, :, atom_count - rim_len :].add(from_above)
    return (
        grad_x,
        lax.psum_scatter(sum_zero, "brick", scatter_dimension=3, tiled=True),
        lax.psum_scatter(
            sum_one.reshape((-1,) + sum_one.shape[2:]), "brick", scatter_dimension=3, tiled=True
        ).reshape(sum_one.shape[:4] + (-1,)),
        lax.psum_scatter(
            sum_two.reshape((-1,) + sum_two.shape[2:]), "brick", scatter_dimension=3, tiled=True
        ).reshape(sum_two.shape[:4] + (-1,)),
    )


def solution(mesh):
    in_specs = (
        P(None, "chan", "brick"),
        P(None, "chan", "brick"),
        P(None, "brick"),
        P("brick"),
        P("brick"),
        P("brick"),
        P("brick"),
        P(None, "chan", None, None),
        P(None, None, "chan", None, None),
        P(None, None, "chan", None, None),
    )
    out_specs = (
        P(None, "chan", "brick"),
        P(None, "chan", None, "brick"),
        P(None, None, "chan", None, "brick"),
        P(None, None, "chan", None, "brick"),
    )
    bricks, shards = mesh.shape["brick"], mesh.shape["chan"]
    fits = bricks == 2 * shards and bricks == 8
    chosen = kernel_body if fits else body
    return jax.shard_map(chosen, mesh=mesh, in_specs=in_specs, out_specs=out_specs, check_vma=False)
```

```python
import functools

import jax
import jax.numpy as jnp
from jax import lax
from jax.experimental import pallas as pl
from jax.experimental.pallas import tpu as pltpu
from jax.sharding import PartitionSpec as P

LANES = 128
VMEM_BYTES = 63 * 1024 * 1024
MESH = pl.DeviceIdType.MESH
NT = (((1,), (1,)), ((), ()))
NN = (((1,), (0,)), ((), ()))


def degree_offset(degree):
    return sum((2 * min(k, 2) + 1) * (2 * k + 1) for k in range(degree))


def rotate_tile(load, wig, store):
    for degree in range(7):
        top = min(degree, 2)
        span = 2 * degree + 1
        offset = degree_offset(degree)
        sums = [None] * (2 * top + 1)
        for column in range(span):
            value = load(degree * degree + column)
            for m in range(2 * top + 1):
                term = wig(offset + m * span + column) * value
                sums[m] = term if sums[m] is None else sums[m] + term
        for m in range(2 * top + 1):
            store(kept_row(degree, m - top), sums[m])


def unrotate_tile(load, wig, store):
    for degree in range(7):
        top = min(degree, 2)
        span = 2 * degree + 1
        offset = degree_offset(degree)
        rows = [load(kept_row(degree, m - top)) for m in range(2 * top + 1)]
        for column in range(span):
            total = None
            for m in range(2 * top + 1):
                term = wig(offset + m * span + column) * rows[m]
                total = term if total is None else total + term
            store(degree * degree + column, total)


def source_onehot(src, rows, rim):
    place = jnp.where(src < rim, src + (rows - rim), src - rim)
    return (lax.broadcasted_iota(jnp.int32, (rows, src.shape[1]), 0) == place).astype(jnp.bfloat16)


def dot(a, b, dims):
    return lax.dot_general(a, b, dims, preferred_element_type=jnp.float32)


def fused_kernel(
    bricks, shards, chan, total, piece, rim, width,
    count_ref, src_ref, dst_ref, scale_ref, wig_ref, cot_ref, x_ref, wz_ref, w1_ref, w2_ref,
    sum_ref, gx_ref,
    wig_in, wz_in, w1_in, w2_in,
    wide, scaled, at_dst, at_src, cot, x_next, x_prev, ext, gathered, grad, edge_in,
    wz, w1, w2, back, full, gx, part, near, far, outgoing, to_next, to_prev, from_next, from_prev,
    local, send_up, send_down, recv_cot, send_x, recv_x, send1, recv1, send2, recv2,
    send_rim, recv_rim,
):
    me = lax.axis_index("brick")
    z = lax.axis_index("chan")
    core = lax.rem(me, 2)
    mine = lax.div(me, 2)
    pairs = bricks // 2
    sibling = me + 1 - 2 * core
    following = lax.rem(me + 1, bricks)
    previous = lax.rem(me + bricks - 1, bricks)
    atoms = x_ref.shape[1]
    slots = src_ref.shape[1]
    copies = [
        pltpu.make_async_copy(source, target, local.at[i])
        for i, (source, target) in enumerate((
            (wig_ref, wig_in), (cot_ref, cot.at[z]), (x_ref, ext.at[:, :atoms]),
            (wz_ref, wz_in), (w1_ref, w1_in), (w2_ref, w2_in),
        ))
    ]
    for copy in copies:
        copy.start()
    coef = x_ref.shape[0] // chan
    f32, bf16 = jnp.float32, jnp.bfloat16

    barrier = pltpu.get_barrier_semaphore()
    for d in range(1, bricks):
        pl.semaphore_signal(
            barrier, inc=1, device_id={"brick": lax.rem(me + d, bricks)}, device_id_type=MESH
        )

    @pl.when(z > 0)
    def _():
        pl.semaphore_signal(barrier, inc=1, device_id={"chan": z - 1}, device_id_type=MESH)

    @pl.when(z < shards - 1)
    def _():
        pl.semaphore_signal(barrier, inc=1, device_id={"chan": z + 1}, device_id_type=MESH)

    ends = jnp.where(z > 0, 1, 0) + jnp.where(z < shards - 1, 1, 0)
    pl.semaphore_wait(barrier, bricks - 1 + ends)

    def remote(src, dst, send, recv, axis, to):
        return pltpu.make_async_remote_copy(
            src_ref=src, dst_ref=dst, send_sem=send, recv_sem=recv,
            device_id={axis: to}, device_id_type=MESH,
        )

    def up(s, src=None):
        src = cot.at[s] if src is None else src
        return remote(src, cot.at[s], send_up.at[s], recv_cot.at[s], "chan", z + 1)

    def down(s, src=None):
        src = cot.at[s] if src is None else src
        return remote(src, cot.at[s], send_down.at[s], recv_cot.at[s], "chan", z - 1)

    @pl.when(z < shards - 1)
    def _():
        up(z, cot_ref).start()

    @pl.when(z > 0)
    def _():
        down(z, cot_ref).start()

    halos = [
        remote(x_ref, x_next, send_x.at[0], recv_x.at[0], "brick", previous),
        remote(x_ref, x_prev, send_x.at[1], recv_x.at[1], "brick", following),
    ]
    for copy in halos:
        copy.start()

    at_dst[...] = (
        lax.broadcasted_iota(jnp.int32, (atoms, slots), 0) == dst_ref[...]
    ).astype(bf16)
    at_src[...] = source_onehot(src_ref[...], 2 * atoms, rim)
    back[...] = jnp.zeros_like(back)
    position = lax.broadcasted_iota(jnp.int32, (1, slots), 1)
    factor = jnp.where(position < count_ref[0], 0.25 * scale_ref[...], 0.0)
    copies[0].wait()
    wide[...] = wig_in[...].astype(f32)
    scaled[...] = wide[...] * factor
    copies[1].wait()

    def rotate_all(values, onehot, entries, out, stride, first):
        def block_step(i, carry):
            cols = pl.ds(pl.multiple_of(i * width, width), width)
            gathered[...] = dot(values(), onehot[:, cols], NN)

            def lanes_step(t, inner):
                near_at = pl.ds(pl.multiple_of(t * LANES, LANES), LANES)
                at = pl.ds(pl.multiple_of(i * width + t * LANES, LANES), LANES)

                def store(row, tile):
                    out[pl.ds(pl.multiple_of(row * stride + first, chan), chan), at] = tile.astype(
                        bf16
                    )

                rotate_tile(
                    lambda c: gathered[c * chan : (c + 1) * chan, near_at],
                    lambda k: entries[k : k + 1, at],
                    store,
                )
                return inner

            lax.fori_loop(0, width // LANES, lanes_step, 0)
            return carry

        lax.fori_loop(0, slots // width, block_step, 0)

    lane = lax.broadcasted_iota(jnp.int32, (1, atoms), 1)

    def arrival(s):
        return remote(cot_ref, cot.at[s], send_up.at[s], recv_cot.at[s], "chan", z)

    def forward(d):
        @pl.when((z - d >= 0) & (z < shards - 1))
        def _():
            arrival(z - d).wait_recv()
            up(z - d).start()

        @pl.when((z + d < shards) & (z > 0))
        def _():
            arrival(z + d).wait_recv()
            down(z + d).start()

    def split_weights():
        for copy in copies[3:]:
            copy.wait()
        for kept, source, lead, high in (
            (wz, wz_in, (), 7), (w1, w1_in, (0,), 6), (w1, w1_in, (1,), 6),
            (w2, w2_in, (0,), 5), (w2, w2_in, (1,), 5),
        ):
            for i in range(high):
                for j in range(high):
                    tile = source[lead + (i, j)]
                    for s in range(shards):
                        kept[
                            lead + (s, slice(i * chan, (i + 1) * chan),
                                    slice(j * chan, (j + 1) * chan))
                        ] = tile[:, s * chan : (s + 1) * chan]
        part[...] = jnp.zeros_like(part)

    def rotate_inputs():
        copies[2].wait()
        for copy in halos:
            copy.wait_recv()
        ext[:, atoms:] = jnp.where(
            lane < rim, x_next[...].astype(f32), x_prev[...].astype(f32)
        ).astype(bf16)
        rotate_all(lambda: ext[...], at_src, wide, edge_in, chan, 0)

    def stage_one(s):
        return remote(
            part.at[2 * s + (1 - core)], near.at[s], send1.at[s], recv1.at[s], "brick", sibling
        )

    def stage_two(s, d):
        return remote(
            outgoing.at[s], far.at[d], send2.at[d], recv2.at[d], "brick", 2 * s + core
        )

    def shard_products(s):
        def split(row, high, value):
            for h in range(2):
                for j in range(high):
                    lines = value[j * chan + h * piece : j * chan + (h + 1) * piece]
                    part[2 * s + h, row + j * piece : row + (j + 1) * piece, : high * chan] = (
                        lines.astype(bf16)
                    )

        split(0, 7, dot(grad[: 7 * chan], edge_in[: 7 * chan], NT))
        row = 7 * piece
        for first, high in ((7, 6), (19, 5)):
            low, middle, top = first * chan, (first + high) * chan, (first + 2 * high) * chan
            grad_plus, grad_minus = grad[low:middle], grad[middle:top]
            in_plus, in_minus = edge_in[low:middle], edge_in[middle:top]
            split(row, high, dot(grad_plus, in_plus, NT) + dot(grad_minus, in_minus, NT))
            row += high * piece
            split(row, high, dot(grad_minus, in_plus, NT) - dot(grad_plus, in_minus, NT))
            row += high * piece
        stage_one(s).start()

        def contract_step(i, carry):
            cols = pl.ds(pl.multiple_of(i * width, width), width)
            back[: 7 * chan, cols] += dot(wz[s], grad[: 7 * chan, cols], NN)
            for w, first, high in ((w1, 7, 6), (w2, 19, 5)):
                low, middle, top = first * chan, (first + high) * chan, (first + 2 * high) * chan
                plus, minus = grad[low:middle, cols], grad[middle:top, cols]
                back[low:middle, cols] += dot(w[0, s], plus, NN) + dot(w[1, s], minus, NN)
                back[middle:top, cols] += dot(w[0, s], minus, NN) - dot(w[1, s], plus, NN)
            return carry

        lax.fori_loop(0, slots // width, contract_step, 0)
        stage_one(s).wait_recv()
        both = part[2 * s + core].astype(f32) + near[s].astype(f32)

        @pl.when(s == mine)
        def _():
            sum_ref[...] = both

        @pl.when(s != mine)
        def _():
            outgoing[s] = both.astype(bf16)
            stage_two(s, lax.rem(s - mine + pairs, pairs)).start()

    def distance_step(d, carry):
        low, high = z - d, z + d

        def side_step(side, inner):
            s = jnp.where(side == 0, low, high)

            @pl.when((s >= 0) & (s < shards) & (d + (1 - side) > 0))
            def _():
                @pl.when((d > 0) & (z == jnp.where(side == 0, shards - 1, 0)))
                def _():
                    arrival(s).wait_recv()

                rotate_all(lambda: cot[s], at_dst, scaled, grad, chan, 0)

                @pl.when(d == 0)
                def _():
                    split_weights()

                @pl.when((side == 0) | (low < 0))
                def _():
                    forward(d + 1)

                @pl.when(d == 0)
                def _():
                    rotate_inputs()

                shard_products(s)

            return inner

        lax.fori_loop(0, 2, side_step, 0)
        return carry

    lax.fori_loop(0, shards, distance_step, 0)

    gx[...] = jnp.zeros_like(gx)

    def back_block(i, carry):
        cols = pl.ds(pl.multiple_of(i * width, width), width)

        def lanes_step(t, inner):
            near_at = pl.ds(pl.multiple_of(t * LANES, LANES), LANES)
            at = pl.ds(pl.multiple_of(i * width + t * LANES, LANES), LANES)

            def store(c, tile):
                full[c * chan : (c + 1) * chan, near_at] = tile.astype(bf16)

            unrotate_tile(
                lambda r: back[r * chan : (r + 1) * chan, at],
                lambda k: wide[k : k + 1, at],
                store,
            )
            return inner

        lax.fori_loop(0, width // LANES, lanes_step, 0)
        gx[: coef * chan] += dot(full[...], at_src[:, cols], NT)
        return carry

    lax.fori_loop(0, slots // width, back_block, 0)

    groups = atoms // rim
    rows = chan // groups
    tile = gx[:, atoms:].reshape(coef + 1, chan, atoms)
    for packed, start in ((to_next, 0), (to_prev, atoms - rim)):
        laid = jnp.zeros((coef + 1, rows, atoms), f32)
        for q in range(groups):
            turn = (q * rim - start) % atoms
            lines = tile[:, q * rows : (q + 1) * rows].reshape(-1, atoms)
            lines = pltpu.roll(lines, turn, 1) if turn else lines
            inside = (lane >= q * rim) & (lane < (q + 1) * rim)
            laid = jnp.where(inside[None], lines.reshape(laid.shape), laid)
        packed[...] = laid.reshape(packed.shape).astype(bf16)
    rims = [
        remote(to_next, from_prev, send_rim.at[0], recv_rim.at[0], "brick", following),
        remote(to_prev, from_next, send_rim.at[1], recv_rim.at[1], "brick", previous),
    ]
    for copy in rims:
        copy.start()
    for d in range(1, pairs):
        stage_two(0, d).wait_recv()
        sum_ref[...] += far[d].astype(f32)
    for copy in rims:
        copy.wait_recv()
    arrived = [from_prev[...].astype(f32), from_next[...].astype(f32)]
    for q in range(groups):
        total_lines = gx[: coef * chan, :atoms].reshape(coef, chan, atoms)[
            :, q * rows : (q + 1) * rows
        ]
        for lines, start in zip(arrived, (0, atoms - rim)):
            turn = (start - q * rim) % atoms
            lines = pltpu.roll(lines, turn, 1) if turn else lines
            inside = (lane >= start) & (lane < start + rim)
            lines = jnp.where(inside, lines, 0.0)
            total_lines = total_lines + lines.reshape(coef + 1, rows, atoms)[:coef]
        gx_ref[:, q * rows : (q + 1) * rows, :] = total_lines

    for copy in halos + rims:
        copy.wait_send()
    for d in range(1, pairs):
        stage_two(0, d).wait_send()
    for s in range(shards):
        stage_one(s).wait_send()

        @pl.when((z < shards - 1) & (s <= z))
        def _():
            up(s).wait_send()

        @pl.when((z > 0) & (s >= z))
        def _():
            down(s).wait_send()


def kernel_body(
    node_x, cotangent, wigner, src_index, dst_index, edge_scale, edge_count, w_zero, w_one, w_two
):
    bricks, shards = lax.axis_size("brick"), lax.axis_size("chan")
    coef, chan, atoms = node_x.shape
    total = w_zero.shape[3]
    piece = total // bricks
    rim = atoms // 4
    slots = src_index.shape[0]
    entries = wigner.shape[0]
    width = 256
    f32, bf16 = jnp.float32, jnp.bfloat16
    pairs = bricks // 2
    rows = (7 + 12 + 10) * piece
    flat = coef * chan
    packed = (coef + 1) * (chan * rim // atoms)

    def vmem(shape, dtype):
        return pltpu.VMEM(shape, dtype)

    def dma(count):
        return pltpu.SemaphoreType.DMA((count,))

    whole = pl.BlockSpec(memory_space=pltpu.VMEM)
    hbm = pl.BlockSpec(memory_space=pltpu.HBM)
    sums, grad_x = pl.pallas_call(
        functools.partial(fused_kernel, bricks, shards, chan, total, piece, rim, width),
        out_shape=(
            jax.ShapeDtypeStruct((rows, 2 * LANES), f32),
            jax.ShapeDtypeStruct((coef, chan, atoms), f32),
        ),
        in_specs=[pl.BlockSpec(memory_space=pltpu.SMEM)] + [whole] * 3 + [hbm] * 6,
        out_specs=(whole, whole),
        scratch_shapes=[
            vmem((entries, slots), bf16), vmem((7, 7, chan, total), bf16),
            vmem((2, 6, 6, chan, total), bf16), vmem((2, 5, 5, chan, total), bf16),
            vmem((entries, slots), f32), vmem((entries, slots), f32),
            vmem((atoms, slots), bf16), vmem((2 * atoms, slots), bf16),
            vmem((shards, flat, atoms), bf16), vmem((flat, atoms), bf16),
            vmem((flat, atoms), bf16), vmem((flat, 2 * atoms), bf16),
            vmem((flat, width), f32), vmem((29 * chan, slots), bf16),
            vmem((29 * chan, slots), bf16), vmem((shards, 7 * chan, 7 * chan), bf16),
            vmem((2, shards, 6 * chan, 6 * chan), bf16),
            vmem((2, shards, 5 * chan, 5 * chan), bf16),
            vmem((29 * chan, slots), f32), vmem((flat, width), bf16),
            vmem((flat + chan, 2 * atoms), f32), vmem((bricks, rows, 2 * LANES), bf16),
            vmem((pairs, rows, 2 * LANES), bf16), vmem((pairs, rows, 2 * LANES), bf16),
            vmem((pairs, rows, 2 * LANES), bf16),
            vmem((packed, atoms), bf16), vmem((packed, atoms), bf16),
            vmem((packed, atoms), bf16), vmem((packed, atoms), bf16),
            dma(6), dma(shards), dma(shards), dma(shards), dma(2), dma(2),
            dma(pairs), dma(pairs), dma(pairs), dma(pairs), dma(2), dma(2),
        ],
        compiler_params=pltpu.CompilerParams(
            vmem_limit_bytes=VMEM_BYTES, collective_id=0, has_side_effects=True
        ),
        name="fused",
    )(
        edge_count, src_index.reshape(1, slots), dst_index.reshape(1, slots),
        edge_scale.reshape(1, slots), wigner, cotangent.reshape(flat, atoms),
        node_x.reshape(flat, atoms), w_zero.transpose(0, 2, 1, 3),
        w_one.transpose(0, 1, 3, 2, 4), w_two.transpose(0, 1, 3, 2, 4),
    )

    def columns_back(first, high):
        block = sums[first : first + high * piece, : high * chan]
        return block.reshape(high, piece, high, chan).transpose(2, 3, 0, 1)

    ends = [0, 7 * piece, 13 * piece, 19 * piece, 24 * piece]
    return (
        grad_x,
        columns_back(ends[0], 7),
        jnp.stack([columns_back(ends[1], 6), columns_back(ends[2], 6)]),
        jnp.stack([columns_back(ends[3], 5), columns_back(ends[4], 5)]),
    )


def padded(x, sides, width):
    for axis, dim in sides:
        devices, length = (lax.axis_size(axis), x.shape[dim])
        up = [(i, (i + 1) % devices) for i in range(devices)]
        down = [(j, i) for i, j in up]
        last = lax.slice_in_dim(x, length - width, length, axis=dim)
        initial = lax.slice_in_dim(x, 0, width, axis=dim)
        before = lax.ppermute(last, axis, up)
        after = lax.ppermute(initial, axis, down)
        x = jnp.concatenate([before, x, after], axis=dim)
    return x


def passed_along(block, axis, distance):
    devices = range(lax.axis_size(axis))
    route = [((i - distance) % len(devices), i) for i in devices]
    return lax.ppermute(block, axis, route)


def kept_row(degree, azimuth):
    if azimuth == 0:
        return degree
    if azimuth == 1:
        return 6 + degree
    if azimuth == -1:
        return 12 + degree
    if azimuth == 2:
        return 17 + degree
    return 22 + degree


def to_edge_frame(values, wigner):
    kept_rows = [None] * 29
    offset = 0
    for degree in range(7):
        max_order = min(degree, 2)
        span_cols = 2 * degree + 1
        for azimuth in range(-max_order, max_order + 1):
            running = jnp.zeros(values.shape[1:], jnp.float32)
            for column in range(span_cols):
                factor = wigner[offset + (azimuth + max_order) * span_cols + column].astype(
                    jnp.float32
                )
                running = running + factor[None, :] * values[degree * degree + column].astype(
                    jnp.float32
                )
            kept_rows[kept_row(degree, azimuth)] = running
        offset += (2 * max_order + 1) * span_cols
    return jnp.stack(kept_rows)


def from_edge_frame(kept_rows, wigner):
    full_rows = []
    offset = 0
    for degree in range(7):
        max_order = min(degree, 2)
        span_cols = 2 * degree + 1
        for column in range(span_cols):
            running = jnp.zeros(kept_rows.shape[1:], jnp.float32)
            for azimuth in range(-max_order, max_order + 1):
                factor = wigner[offset + (azimuth + max_order) * span_cols + column].astype(
                    jnp.float32
                )
                running = running + factor[None, :] * kept_rows[kept_row(degree, azimuth)]
            full_rows.append(running)
        offset += (2 * max_order + 1) * span_cols
    return jnp.stack(full_rows)


def contract(weights, grads):
    return lax.dot_general(
        weights, grads, (((2, 3), (0, 1)), ((), ())), preferred_element_type=jnp.float32
    )


def outer(inputs, grads):
    return lax.dot_general(
        inputs, grads, (((2,), (2,)), ((), ())), preferred_element_type=jnp.float32
    )


def so2_back(w_zero, w_one, w_two, edge_grad, edge_in):
    back_rows = [contract(w_zero, edge_grad[0:7])]
    term_zero = outer(edge_in[0:7], edge_grad[0:7])
    weight_terms = []
    for weights, bottom, middle, ceiling in ((w_one, 7, 13, 19), (w_two, 19, 24, 29)):
        grad_plus = edge_grad[bottom:middle]
        grad_minus = edge_grad[middle:ceiling]
        in_plus = edge_in[bottom:middle]
        in_minus = edge_in[middle:ceiling]
        back_rows.append(contract(weights[0], grad_plus) + contract(weights[1], grad_minus))
        back_rows.append(contract(weights[0], grad_minus) - contract(weights[1], grad_plus))
        weight_terms.append(
            jnp.stack(
                [
                    outer(in_plus, grad_plus) + outer(in_minus, grad_minus),
                    outer(in_plus, grad_minus) - outer(in_minus, grad_plus),
                ]
            )
        )
    return (jnp.concatenate(back_rows, axis=0), term_zero, weight_terms[0], weight_terms[1])


def add_columns(summed, term, first_col, axis_dim):
    current = lax.dynamic_slice_in_dim(summed, first_col, term.shape[axis_dim], axis_dim)
    return lax.dynamic_update_slice_in_dim(summed, current + term, first_col, axis_dim)


def body(
    node_x, cotangent, wigner, src_index, dst_index, edge_scale, edge_count, w_zero, w_one, w_two
):
    atom_count = node_x.shape[2]
    own_chan = node_x.shape[1]
    coef_count = node_x.shape[0]
    chan_total = w_zero.shape[3]
    rim_len = atom_count // 4
    slot_count = src_index.shape[0]
    block_len = min(512, slot_count)
    live_count = edge_count[0]
    padded_len = atom_count + 2 * rim_len
    extended = padded(node_x, (("brick", 2),), rim_len)
    at_source = jnp.take(extended, src_index, axis=2)
    edge_in = to_edge_frame(at_source, wigner).astype(jnp.bfloat16)
    block_total = slot_count // block_len
    initial = (
        jnp.zeros((29, own_chan, slot_count), jnp.float32),
        jnp.zeros(w_zero.shape[:3] + (chan_total,), jnp.float32),
        jnp.zeros(w_one.shape[:4] + (chan_total,), jnp.float32),
        jnp.zeros(w_two.shape[:4] + (chan_total,), jnp.float32),
    )
    full_grad = lax.all_gather(cotangent, "chan", axis=1, tiled=True)

    def block_step(block_index, running):
        edge_back, sum_zero, sum_one, sum_two = running
        begin_at = block_index * block_len
        dst_block = lax.dynamic_slice_in_dim(dst_index, begin_at, block_len)
        wig_block = lax.dynamic_slice_in_dim(wigner, begin_at, block_len, 1)
        scale_block = lax.dynamic_slice_in_dim(edge_scale, begin_at, block_len)
        position = begin_at + lax.iota(jnp.int32, block_len)
        factor = jnp.where(position < live_count, 0.25 * scale_block, 0.0)
        at_dest = jnp.take(full_grad, dst_block, axis=2)
        edge_grad = (to_edge_frame(at_dest, wig_block) * factor).astype(jnp.bfloat16)
        edge_block = lax.dynamic_slice_in_dim(edge_in, begin_at, block_len, 2)
        back_rows, term_zero, term_one, term_two = so2_back(
            w_zero, w_one, w_two, edge_grad, edge_block
        )
        edge_back = add_columns(edge_back, back_rows, begin_at, 2)
        sum_zero = add_columns(sum_zero, term_zero, 0, 3)
        sum_one = add_columns(sum_one, term_one, 0, 4)
        sum_two = add_columns(sum_two, term_two, 0, 4)
        return (edge_back, sum_zero, sum_one, sum_two)

    folded = lax.fori_loop(0, block_total, block_step, initial)
    edge_back, sum_zero, sum_one, sum_two = folded

    def back_step(block_index, summed):
        begin_at = block_index * block_len
        kept_rows = lax.dynamic_slice_in_dim(edge_back, begin_at, block_len, 2)
        wig_block = lax.dynamic_slice_in_dim(wigner, begin_at, block_len, 1)
        src_block = lax.dynamic_slice_in_dim(src_index, begin_at, block_len)
        full_rows = from_edge_frame(kept_rows, wig_block)
        onehot = (src_block[:, None] == lax.iota(jnp.int32, padded_len)[None, :]).astype(
            jnp.bfloat16
        )
        high_part = full_rows.astype(jnp.bfloat16)
        rest = full_rows - high_part.astype(jnp.float32)
        low_part = rest.astype(jnp.bfloat16)
        dims = (((2,), (0,)), ((), ()))
        summed = summed + lax.dot_general(
            high_part, onehot, dims, preferred_element_type=jnp.float32
        )
        return summed + lax.dot_general(low_part, onehot, dims, preferred_element_type=jnp.float32)

    grad_ext = lax.fori_loop(
        0, block_total, back_step, jnp.zeros((coef_count, own_chan, padded_len), jnp.float32)
    )
    own_part = grad_ext[:, :, rim_len : rim_len + atom_count]
    from_above = passed_along(grad_ext[:, :, :rim_len], "brick", -1)
    from_below = passed_along(grad_ext[:, :, rim_len + atom_count :], "brick", 1)
    own_part = own_part.at[:, :, :rim_len].add(from_below)
    grad_x = own_part.at[:, :, atom_count - rim_len :].add(from_above)
    return (
        grad_x,
        lax.psum_scatter(sum_zero, "brick", scatter_dimension=3, tiled=True),
        lax.psum_scatter(
            sum_one.reshape((-1,) + sum_one.shape[2:]), "brick", scatter_dimension=3, tiled=True
        ).reshape(sum_one.shape[:4] + (-1,)),
        lax.psum_scatter(
            sum_two.reshape((-1,) + sum_two.shape[2:]), "brick", scatter_dimension=3, tiled=True
        ).reshape(sum_two.shape[:4] + (-1,)),
    )


def solution(mesh):
    in_specs = (
        P(None, "chan", "brick"),
        P(None, "chan", "brick"),
        P(None, "brick"),
        P("brick"),
        P("brick"),
        P("brick"),
        P("brick"),
        P(None, "chan", None, None),
        P(None, None, "chan", None, None),
        P(None, None, "chan", None, None),
    )
    out_specs = (
        P(None, "chan", "brick"),
        P(None, "chan", None, "brick"),
        P(None, None, "chan", None, "brick"),
        P(None, None, "chan", None, "brick"),
    )
    bricks, shards = mesh.shape["brick"], mesh.shape["chan"]
    fits = bricks == 2 * shards and bricks == 8
    chosen = kernel_body if fits else body
    return jax.shard_map(chosen, mesh=mesh, in_specs=in_specs, out_specs=out_specs, check_vma=False)
```

```python
import functools

import jax
import jax.numpy as jnp
from jax import lax
from jax.experimental import pallas as pl
from jax.experimental.pallas import tpu as pltpu
from jax.sharding import PartitionSpec as P

LANES = 128
VMEM_BYTES = 63 * 1024 * 1024
MESH = pl.DeviceIdType.MESH
NT = (((1,), (1,)), ((), ()))
NN = (((1,), (0,)), ((), ()))


def degree_offset(degree):
    return sum((2 * min(k, 2) + 1) * (2 * k + 1) for k in range(degree))


def rotate_tile(load, wig, store):
    for degree in range(7):
        top = min(degree, 2)
        span = 2 * degree + 1
        offset = degree_offset(degree)
        sums = [None] * (2 * top + 1)
        for column in range(span):
            value = load(degree * degree + column)
            for m in range(2 * top + 1):
                term = wig(offset + m * span + column) * value
                sums[m] = term if sums[m] is None else sums[m] + term
        for m in range(2 * top + 1):
            store(kept_row(degree, m - top), sums[m])


def unrotate_tile(load, wig, store):
    for degree in range(7):
        top = min(degree, 2)
        span = 2 * degree + 1
        offset = degree_offset(degree)
        rows = [load(kept_row(degree, m - top)) for m in range(2 * top + 1)]
        for column in range(span):
            total = None
            for m in range(2 * top + 1):
                term = wig(offset + m * span + column) * rows[m]
                total = term if total is None else total + term
            store(degree * degree + column, total)


def source_onehot(src, rows, rim):
    place = jnp.where(src < rim, src + (rows - rim), src - rim)
    return (lax.broadcasted_iota(jnp.int32, (rows, src.shape[1]), 0) == place).astype(jnp.bfloat16)


def dot(a, b, dims):
    return lax.dot_general(a, b, dims, preferred_element_type=jnp.float32)


def fused_kernel(
    bricks, shards, chan, total, piece, rim, width,
    count_ref, src_ref, dst_ref, scale_ref, wig_ref, cot_ref, x_ref, wz_ref, w1_ref, w2_ref,
    zero_ref, one_ref, two_ref, gx_ref,
    sum_ref, wig_in, wz_in, w1_in, w2_in,
    wide, scaled, at_dst, at_src, cot, x_next, x_prev, ext, gathered, grad, edge_in,
    wz, w1, w2, back, full, gx, part, near, far, outgoing, to_next, to_prev, from_next, from_prev,
    local, send_up, send_down, recv_cot, send_x, recv_x, send1, recv1, send2, recv2,
    send_rim, recv_rim,
):
    me = lax.axis_index("brick")
    z = lax.axis_index("chan")
    core = lax.rem(me, 2)
    mine = lax.div(me, 2)
    pairs = bricks // 2
    sibling = me + 1 - 2 * core
    following = lax.rem(me + 1, bricks)
    previous = lax.rem(me + bricks - 1, bricks)
    atoms = x_ref.shape[1]
    slots = src_ref.shape[1]
    copies = [
        pltpu.make_async_copy(source, target, local.at[i])
        for i, (source, target) in enumerate((
            (wig_ref, wig_in), (cot_ref, cot.at[z]), (x_ref, ext.at[:, :atoms]),
            (wz_ref, wz_in), (w1_ref, w1_in), (w2_ref, w2_in),
        ))
    ]
    for copy in copies:
        copy.start()
    coef = x_ref.shape[0] // chan
    f32, bf16 = jnp.float32, jnp.bfloat16

    barrier = pltpu.get_barrier_semaphore()
    for d in range(1, bricks):
        pl.semaphore_signal(
            barrier, inc=1, device_id={"brick": lax.rem(me + d, bricks)}, device_id_type=MESH
        )

    @pl.when(z > 0)
    def _():
        pl.semaphore_signal(barrier, inc=1, device_id={"chan": z - 1}, device_id_type=MESH)

    @pl.when(z < shards - 1)
    def _():
        pl.semaphore_signal(barrier, inc=1, device_id={"chan": z + 1}, device_id_type=MESH)

    ends = jnp.where(z > 0, 1, 0) + jnp.where(z < shards - 1, 1, 0)
    pl.semaphore_wait(barrier, bricks - 1 + ends)

    def remote(src, dst, send, recv, axis, to):
        return pltpu.make_async_remote_copy(
            src_ref=src, dst_ref=dst, send_sem=send, recv_sem=recv,
            device_id={axis: to}, device_id_type=MESH,
        )

    def up(s, src=None):
        src = cot.at[s] if src is None else src
        return remote(src, cot.at[s], send_up.at[s], recv_cot.at[s], "chan", z + 1)

    def down(s, src=None):
        src = cot.at[s] if src is None else src
        return remote(src, cot.at[s], send_down.at[s], recv_cot.at[s], "chan", z - 1)

    @pl.when(z < shards - 1)
    def _():
        up(z, cot_ref).start()

    @pl.when(z > 0)
    def _():
        down(z, cot_ref).start()

    halos = [
        remote(x_ref, x_next, send_x.at[0], recv_x.at[0], "brick", previous),
        remote(x_ref, x_prev, send_x.at[1], recv_x.at[1], "brick", following),
    ]
    for copy in halos:
        copy.start()

    at_dst[...] = (
        lax.broadcasted_iota(jnp.int32, (atoms, slots), 0) == dst_ref[...]
    ).astype(bf16)
    at_src[...] = source_onehot(src_ref[...], 2 * atoms, rim)
    back[...] = jnp.zeros_like(back)
    position = lax.broadcasted_iota(jnp.int32, (1, slots), 1)
    factor = jnp.where(position < count_ref[0], 0.25 * scale_ref[...], 0.0)
    copies[0].wait()
    wide[...] = wig_in[...].astype(f32)
    scaled[...] = wide[...] * factor
    copies[1].wait()

    def rotate_all(values, onehot, entries, out, stride, first):
        def block_step(i, carry):
            cols = pl.ds(pl.multiple_of(i * width, width), width)
            gathered[...] = dot(values(), onehot[:, cols], NN)

            def lanes_step(t, inner):
                near_at = pl.ds(pl.multiple_of(t * LANES, LANES), LANES)
                at = pl.ds(pl.multiple_of(i * width + t * LANES, LANES), LANES)

                def store(row, tile):
                    out[pl.ds(pl.multiple_of(row * stride + first, chan), chan), at] = tile.astype(
                        bf16
                    )

                rotate_tile(
                    lambda c: gathered[c * chan : (c + 1) * chan, near_at],
                    lambda k: entries[k : k + 1, at],
                    store,
                )
                return inner

            lax.fori_loop(0, width // LANES, lanes_step, 0)
            return carry

        lax.fori_loop(0, slots // width, block_step, 0)

    lane = lax.broadcasted_iota(jnp.int32, (1, atoms), 1)

    def arrival(s):
        return remote(cot_ref, cot.at[s], send_up.at[s], recv_cot.at[s], "chan", z)

    def forward(d):
        @pl.when((z - d >= 0) & (z < shards - 1))
        def _():
            arrival(z - d).wait_recv()
            up(z - d).start()

        @pl.when((z + d < shards) & (z > 0))
        def _():
            arrival(z + d).wait_recv()
            down(z + d).start()

    def split_weights():
        for copy in copies[3:]:
            copy.wait()
        for kept, source, lead, high in (
            (wz, wz_in, (), 7), (w1, w1_in, (0,), 6), (w1, w1_in, (1,), 6),
            (w2, w2_in, (0,), 5), (w2, w2_in, (1,), 5),
        ):
            for i in range(high):
                for j in range(high):
                    tile = source[lead + (i, j)]
                    for s in range(shards):
                        kept[
                            lead + (s, slice(i * chan, (i + 1) * chan),
                                    slice(j * chan, (j + 1) * chan))
                        ] = tile[:, s * chan : (s + 1) * chan]
        part[...] = jnp.zeros_like(part)

    def rotate_inputs():
        copies[2].wait()
        for copy in halos:
            copy.wait_recv()
        ext[:, atoms:] = jnp.where(
            lane < rim, x_next[...].astype(f32), x_prev[...].astype(f32)
        ).astype(bf16)
        rotate_all(lambda: ext[...], at_src, wide, edge_in, chan, 0)

    def stage_one(s):
        return remote(
            part.at[2 * s + (1 - core)], near.at[s], send1.at[s], recv1.at[s], "brick", sibling
        )

    def stage_two(s, d):
        return remote(
            outgoing.at[s], far.at[d], send2.at[d], recv2.at[d], "brick", 2 * s + core
        )

    def shard_products(s):
        def split(row, high, value):
            for h in range(2):
                for j in range(high):
                    lines = value[j * chan + h * piece : j * chan + (h + 1) * piece]
                    part[2 * s + h, row + j * piece : row + (j + 1) * piece, : high * chan] = (
                        lines.astype(bf16)
                    )

        split(0, 7, dot(grad[: 7 * chan], edge_in[: 7 * chan], NT))
        row = 7 * piece
        for first, high in ((7, 6), (19, 5)):
            low, middle, top = first * chan, (first + high) * chan, (first + 2 * high) * chan
            grad_plus, grad_minus = grad[low:middle], grad[middle:top]
            in_plus, in_minus = edge_in[low:middle], edge_in[middle:top]
            split(row, high, dot(grad_plus, in_plus, NT) + dot(grad_minus, in_minus, NT))
            row += high * piece
            split(row, high, dot(grad_minus, in_plus, NT) - dot(grad_plus, in_minus, NT))
            row += high * piece
        stage_one(s).start()

        def contract_step(i, carry):
            cols = pl.ds(pl.multiple_of(i * width, width), width)
            back[: 7 * chan, cols] += dot(wz[s], grad[: 7 * chan, cols], NN)
            for w, first, high in ((w1, 7, 6), (w2, 19, 5)):
                low, middle, top = first * chan, (first + high) * chan, (first + 2 * high) * chan
                plus, minus = grad[low:middle, cols], grad[middle:top, cols]
                back[low:middle, cols] += dot(w[0, s], plus, NN) + dot(w[1, s], minus, NN)
                back[middle:top, cols] += dot(w[0, s], minus, NN) - dot(w[1, s], plus, NN)
            return carry

        lax.fori_loop(0, slots // width, contract_step, 0)
        stage_one(s).wait_recv()
        both = part[2 * s + core].astype(f32) + near[s].astype(f32)

        @pl.when(s == mine)
        def _():
            sum_ref[...] = both

        @pl.when(s != mine)
        def _():
            outgoing[s] = both.astype(bf16)
            stage_two(s, lax.rem(s - mine + pairs, pairs)).start()

    def distance_step(d, carry):
        low, high = z - d, z + d

        def side_step(side, inner):
            s = jnp.where(side == 0, low, high)

            @pl.when((s >= 0) & (s < shards) & (d + (1 - side) > 0))
            def _():
                @pl.when((d > 0) & (z == jnp.where(side == 0, shards - 1, 0)))
                def _():
                    arrival(s).wait_recv()

                rotate_all(lambda: cot[s], at_dst, scaled, grad, chan, 0)

                @pl.when(d == 0)
                def _():
                    split_weights()

                @pl.when((side == 0) | (low < 0))
                def _():
                    forward(d + 1)

                @pl.when(d == 0)
                def _():
                    rotate_inputs()

                shard_products(s)

            return inner

        lax.fori_loop(0, 2, side_step, 0)
        return carry

    lax.fori_loop(0, shards, distance_step, 0)

    gx[...] = jnp.zeros_like(gx)

    def back_block(i, carry):
        cols = pl.ds(pl.multiple_of(i * width, width), width)

        def lanes_step(t, inner):
            near_at = pl.ds(pl.multiple_of(t * LANES, LANES), LANES)
            at = pl.ds(pl.multiple_of(i * width + t * LANES, LANES), LANES)

            def store(c, tile):
                full[c * chan : (c + 1) * chan, near_at] = tile.astype(bf16)

            unrotate_tile(
                lambda r: back[r * chan : (r + 1) * chan, at],
                lambda k: wide[k : k + 1, at],
                store,
            )
            return inner

        lax.fori_loop(0, width // LANES, lanes_step, 0)
        gx[: coef * chan] += dot(full[...], at_src[:, cols], NT)
        return carry

    lax.fori_loop(0, slots // width, back_block, 0)

    groups = atoms // rim
    rows = chan // groups
    tile = gx[:, atoms:].reshape(coef + 1, chan, atoms)
    for packed, start in ((to_next, 0), (to_prev, atoms - rim)):
        laid = jnp.zeros((coef + 1, rows, atoms), f32)
        for q in range(groups):
            turn = (q * rim - start) % atoms
            lines = tile[:, q * rows : (q + 1) * rows].reshape(-1, atoms)
            lines = pltpu.roll(lines, turn, 1) if turn else lines
            inside = (lane >= q * rim) & (lane < (q + 1) * rim)
            laid = jnp.where(inside[None], lines.reshape(laid.shape), laid)
        packed[...] = laid.reshape(packed.shape).astype(bf16)
    rims = [
        remote(to_next, from_prev, send_rim.at[0], recv_rim.at[0], "brick", following),
        remote(to_prev, from_next, send_rim.at[1], recv_rim.at[1], "brick", previous),
    ]
    for copy in rims:
        copy.start()
    for d in range(1, pairs):
        stage_two(0, d).wait_recv()
        sum_ref[...] += far[d].astype(f32)
    zero_ref[...] = sum_ref[: 7 * piece, : 7 * chan]
    for k in range(2):
        low = (7 + 6 * k) * piece
        one_ref[k] = sum_ref[low : low + 6 * piece, : 6 * chan]
        low = (19 + 5 * k) * piece
        two_ref[k] = sum_ref[low : low + 5 * piece, : 5 * chan]
    for copy in rims:
        copy.wait_recv()
    arrived = [from_prev[...].astype(f32), from_next[...].astype(f32)]
    for q in range(groups):
        total_lines = gx[: coef * chan, :atoms].reshape(coef, chan, atoms)[
            :, q * rows : (q + 1) * rows
        ]
        for lines, start in zip(arrived, (0, atoms - rim)):
            turn = (start - q * rim) % atoms
            lines = pltpu.roll(lines, turn, 1) if turn else lines
            inside = (lane >= start) & (lane < start + rim)
            lines = jnp.where(inside, lines, 0.0)
            total_lines = total_lines + lines.reshape(coef + 1, rows, atoms)[:coef]
        gx_ref[:, q * rows : (q + 1) * rows, :] = total_lines

    for copy in halos + rims:
        copy.wait_send()
    for d in range(1, pairs):
        stage_two(0, d).wait_send()
    for s in range(shards):
        stage_one(s).wait_send()

        @pl.when((z < shards - 1) & (s <= z))
        def _():
            up(s).wait_send()

        @pl.when((z > 0) & (s >= z))
        def _():
            down(s).wait_send()


def kernel_body(
    node_x, cotangent, wigner, src_index, dst_index, edge_scale, edge_count, w_zero, w_one, w_two
):
    bricks, shards = lax.axis_size("brick"), lax.axis_size("chan")
    coef, chan, atoms = node_x.shape
    total = w_zero.shape[3]
    piece = total // bricks
    rim = atoms // 4
    slots = src_index.shape[0]
    entries = wigner.shape[0]
    width = 256
    f32, bf16 = jnp.float32, jnp.bfloat16
    pairs = bricks // 2
    rows = (7 + 12 + 10) * piece
    flat = coef * chan
    packed = (coef + 1) * (chan * rim // atoms)

    def vmem(shape, dtype):
        return pltpu.VMEM(shape, dtype)

    def dma(count):
        return pltpu.SemaphoreType.DMA((count,))

    whole = pl.BlockSpec(memory_space=pltpu.VMEM)
    hbm = pl.BlockSpec(memory_space=pltpu.HBM)
    zero, one, two, grad_x = pl.pallas_call(
        functools.partial(fused_kernel, bricks, shards, chan, total, piece, rim, width),
        out_shape=(
            jax.ShapeDtypeStruct((7 * piece, 7 * chan), f32),
            jax.ShapeDtypeStruct((2, 6 * piece, 6 * chan), f32),
            jax.ShapeDtypeStruct((2, 5 * piece, 5 * chan), f32),
            jax.ShapeDtypeStruct((coef, chan, atoms), f32),
        ),
        in_specs=[pl.BlockSpec(memory_space=pltpu.SMEM)] + [whole] * 3 + [hbm] * 6,
        out_specs=(whole, whole, whole, whole),
        scratch_shapes=[
            vmem((rows, 2 * LANES), f32), vmem((entries, slots), bf16), vmem((7, 7, chan, total), bf16),
            vmem((2, 6, 6, chan, total), bf16), vmem((2, 5, 5, chan, total), bf16),
            vmem((entries, slots), f32), vmem((entries, slots), f32),
            vmem((atoms, slots), bf16), vmem((2 * atoms, slots), bf16),
            vmem((shards, flat, atoms), bf16), vmem((flat, atoms), bf16),
            vmem((flat, atoms), bf16), vmem((flat, 2 * atoms), bf16),
            vmem((flat, width), f32), vmem((29 * chan, slots), bf16),
            vmem((29 * chan, slots), bf16), vmem((shards, 7 * chan, 7 * chan), bf16),
            vmem((2, shards, 6 * chan, 6 * chan), bf16),
            vmem((2, shards, 5 * chan, 5 * chan), bf16),
            vmem((29 * chan, slots), f32), vmem((flat, width), bf16),
            vmem((flat + chan, 2 * atoms), f32), vmem((bricks, rows, 2 * LANES), bf16),
            vmem((pairs, rows, 2 * LANES), bf16), vmem((pairs, rows, 2 * LANES), bf16),
            vmem((pairs, rows, 2 * LANES), bf16),
            vmem((packed, atoms), bf16), vmem((packed, atoms), bf16),
            vmem((packed, atoms), bf16), vmem((packed, atoms), bf16),
            dma(6), dma(shards), dma(shards), dma(shards), dma(2), dma(2),
            dma(pairs), dma(pairs), dma(pairs), dma(pairs), dma(2), dma(2),
        ],
        compiler_params=pltpu.CompilerParams(
            vmem_limit_bytes=VMEM_BYTES, collective_id=0, has_side_effects=True
        ),
        name="fused",
    )(
        edge_count, src_index.reshape(1, slots), dst_index.reshape(1, slots),
        edge_scale.reshape(1, slots), wigner, cotangent.reshape(flat, atoms),
        node_x.reshape(flat, atoms), w_zero.transpose(0, 2, 1, 3),
        w_one.transpose(0, 1, 3, 2, 4), w_two.transpose(0, 1, 3, 2, 4),
    )

    def columns_back(sums, high):
        lead = sums.shape[:-2]
        sums = sums.reshape(lead + (high, piece, high, chan))
        return jnp.moveaxis(sums, (-2, -1), (-4, -3))

    return (grad_x, columns_back(zero, 7), columns_back(one, 6), columns_back(two, 5))


def padded(x, sides, width):
    for axis, dim in sides:
        devices, length = (lax.axis_size(axis), x.shape[dim])
        up = [(i, (i + 1) % devices) for i in range(devices)]
        down = [(j, i) for i, j in up]
        last = lax.slice_in_dim(x, length - width, length, axis=dim)
        initial = lax.slice_in_dim(x, 0, width, axis=dim)
        before = lax.ppermute(last, axis, up)
        after = lax.ppermute(initial, axis, down)
        x = jnp.concatenate([before, x, after], axis=dim)
    return x


def passed_along(block, axis, distance):
    devices = range(lax.axis_size(axis))
    route = [((i - distance) % len(devices), i) for i in devices]
    return lax.ppermute(block, axis, route)


def kept_row(degree, azimuth):
    if azimuth == 0:
        return degree
    if azimuth == 1:
        return 6 + degree
    if azimuth == -1:
        return 12 + degree
    if azimuth == 2:
        return 17 + degree
    return 22 + degree


def to_edge_frame(values, wigner):
    kept_rows = [None] * 29
    offset = 0
    for degree in range(7):
        max_order = min(degree, 2)
        span_cols = 2 * degree + 1
        for azimuth in range(-max_order, max_order + 1):
            running = jnp.zeros(values.shape[1:], jnp.float32)
            for column in range(span_cols):
                factor = wigner[offset + (azimuth + max_order) * span_cols + column].astype(
                    jnp.float32
                )
                running = running + factor[None, :] * values[degree * degree + column].astype(
                    jnp.float32
                )
            kept_rows[kept_row(degree, azimuth)] = running
        offset += (2 * max_order + 1) * span_cols
    return jnp.stack(kept_rows)


def from_edge_frame(kept_rows, wigner):
    full_rows = []
    offset = 0
    for degree in range(7):
        max_order = min(degree, 2)
        span_cols = 2 * degree + 1
        for column in range(span_cols):
            running = jnp.zeros(kept_rows.shape[1:], jnp.float32)
            for azimuth in range(-max_order, max_order + 1):
                factor = wigner[offset + (azimuth + max_order) * span_cols + column].astype(
                    jnp.float32
                )
                running = running + factor[None, :] * kept_rows[kept_row(degree, azimuth)]
            full_rows.append(running)
        offset += (2 * max_order + 1) * span_cols
    return jnp.stack(full_rows)


def contract(weights, grads):
    return lax.dot_general(
        weights, grads, (((2, 3), (0, 1)), ((), ())), preferred_element_type=jnp.float32
    )


def outer(inputs, grads):
    return lax.dot_general(
        inputs, grads, (((2,), (2,)), ((), ())), preferred_element_type=jnp.float32
    )


def so2_back(w_zero, w_one, w_two, edge_grad, edge_in):
    back_rows = [contract(w_zero, edge_grad[0:7])]
    term_zero = outer(edge_in[0:7], edge_grad[0:7])
    weight_terms = []
    for weights, bottom, middle, ceiling in ((w_one, 7, 13, 19), (w_two, 19, 24, 29)):
        grad_plus = edge_grad[bottom:middle]
        grad_minus = edge_grad[middle:ceiling]
        in_plus = edge_in[bottom:middle]
        in_minus = edge_in[middle:ceiling]
        back_rows.append(contract(weights[0], grad_plus) + contract(weights[1], grad_minus))
        back_rows.append(contract(weights[0], grad_minus) - contract(weights[1], grad_plus))
        weight_terms.append(
            jnp.stack(
                [
                    outer(in_plus, grad_plus) + outer(in_minus, grad_minus),
                    outer(in_plus, grad_minus) - outer(in_minus, grad_plus),
                ]
            )
        )
    return (jnp.concatenate(back_rows, axis=0), term_zero, weight_terms[0], weight_terms[1])


def add_columns(summed, term, first_col, axis_dim):
    current = lax.dynamic_slice_in_dim(summed, first_col, term.shape[axis_dim], axis_dim)
    return lax.dynamic_update_slice_in_dim(summed, current + term, first_col, axis_dim)


def body(
    node_x, cotangent, wigner, src_index, dst_index, edge_scale, edge_count, w_zero, w_one, w_two
):
    atom_count = node_x.shape[2]
    own_chan = node_x.shape[1]
    coef_count = node_x.shape[0]
    chan_total = w_zero.shape[3]
    rim_len = atom_count // 4
    slot_count = src_index.shape[0]
    block_len = min(512, slot_count)
    live_count = edge_count[0]
    padded_len = atom_count + 2 * rim_len
    extended = padded(node_x, (("brick", 2),), rim_len)
    at_source = jnp.take(extended, src_index, axis=2)
    edge_in = to_edge_frame(at_source, wigner).astype(jnp.bfloat16)
    block_total = slot_count // block_len
    initial = (
        jnp.zeros((29, own_chan, slot_count), jnp.float32),
        jnp.zeros(w_zero.shape[:3] + (chan_total,), jnp.float32),
        jnp.zeros(w_one.shape[:4] + (chan_total,), jnp.float32),
        jnp.zeros(w_two.shape[:4] + (chan_total,), jnp.float32),
    )
    full_grad = lax.all_gather(cotangent, "chan", axis=1, tiled=True)

    def block_step(block_index, running):
        edge_back, sum_zero, sum_one, sum_two = running
        begin_at = block_index * block_len
        dst_block = lax.dynamic_slice_in_dim(dst_index, begin_at, block_len)
        wig_block = lax.dynamic_slice_in_dim(wigner, begin_at, block_len, 1)
        scale_block = lax.dynamic_slice_in_dim(edge_scale, begin_at, block_len)
        position = begin_at + lax.iota(jnp.int32, block_len)
        factor = jnp.where(position < live_count, 0.25 * scale_block, 0.0)
        at_dest = jnp.take(full_grad, dst_block, axis=2)
        edge_grad = (to_edge_frame(at_dest, wig_block) * factor).astype(jnp.bfloat16)
        edge_block = lax.dynamic_slice_in_dim(edge_in, begin_at, block_len, 2)
        back_rows, term_zero, term_one, term_two = so2_back(
            w_zero, w_one, w_two, edge_grad, edge_block
        )
        edge_back = add_columns(edge_back, back_rows, begin_at, 2)
        sum_zero = add_columns(sum_zero, term_zero, 0, 3)
        sum_one = add_columns(sum_one, term_one, 0, 4)
        sum_two = add_columns(sum_two, term_two, 0, 4)
        return (edge_back, sum_zero, sum_one, sum_two)

    folded = lax.fori_loop(0, block_total, block_step, initial)
    edge_back, sum_zero, sum_one, sum_two = folded

    def back_step(block_index, summed):
        begin_at = block_index * block_len
        kept_rows = lax.dynamic_slice_in_dim(edge_back, begin_at, block_len, 2)
        wig_block = lax.dynamic_slice_in_dim(wigner, begin_at, block_len, 1)
        src_block = lax.dynamic_slice_in_dim(src_index, begin_at, block_len)
        full_rows = from_edge_frame(kept_rows, wig_block)
        onehot = (src_block[:, None] == lax.iota(jnp.int32, padded_len)[None, :]).astype(
            jnp.bfloat16
        )
        high_part = full_rows.astype(jnp.bfloat16)
        rest = full_rows - high_part.astype(jnp.float32)
        low_part = rest.astype(jnp.bfloat16)
        dims = (((2,), (0,)), ((), ()))
        summed = summed + lax.dot_general(
            high_part, onehot, dims, preferred_element_type=jnp.float32
        )
        return summed + lax.dot_general(low_part, onehot, dims, preferred_element_type=jnp.float32)

    grad_ext = lax.fori_loop(
        0, block_total, back_step, jnp.zeros((coef_count, own_chan, padded_len), jnp.float32)
    )
    own_part = grad_ext[:, :, rim_len : rim_len + atom_count]
    from_above = passed_along(grad_ext[:, :, :rim_len], "brick", -1)
    from_below = passed_along(grad_ext[:, :, rim_len + atom_count :], "brick", 1)
    own_part = own_part.at[:, :, :rim_len].add(from_below)
    grad_x = own_part.at[:, :, atom_count - rim_len :].add(from_above)
    return (
        grad_x,
        lax.psum_scatter(sum_zero, "brick", scatter_dimension=3, tiled=True),
        lax.psum_scatter(
            sum_one.reshape((-1,) + sum_one.shape[2:]), "brick", scatter_dimension=3, tiled=True
        ).reshape(sum_one.shape[:4] + (-1,)),
        lax.psum_scatter(
            sum_two.reshape((-1,) + sum_two.shape[2:]), "brick", scatter_dimension=3, tiled=True
        ).reshape(sum_two.shape[:4] + (-1,)),
    )


def solution(mesh):
    in_specs = (
        P(None, "chan", "brick"),
        P(None, "chan", "brick"),
        P(None, "brick"),
        P("brick"),
        P("brick"),
        P("brick"),
        P("brick"),
        P(None, "chan", None, None),
        P(None, None, "chan", None, None),
        P(None, None, "chan", None, None),
    )
    out_specs = (
        P(None, "chan", "brick"),
        P(None, "chan", None, "brick"),
        P(None, None, "chan", None, "brick"),
        P(None, None, "chan", None, "brick"),
    )
    bricks, shards = mesh.shape["brick"], mesh.shape["chan"]
    fits = bricks == 2 * shards and bricks == 8
    chosen = kernel_body if fits else body
    return jax.shard_map(chosen, mesh=mesh, in_specs=in_specs, out_specs=out_specs, check_vma=False)
```
